256 devices in a mesh: brick: 128 (over z, x_lo, y, core), orb: 2 (over x_hi).
Axes of the slice: x: 4 (x_hi: 2, x_lo: 2; x = x_hi * 2 + x_lo), y: 4, z: 8, core: 2. Of those that a mesh axis runs over, the one named last changes fastest.
Arguments:
- orbitals: float32 [64, 128, 6, 6, 128], P('orb', 'brick'), may hold values from -24 to 24
- potential: float32 [128, 6, 6, 128], P('brick'), may hold values from 0 to 2
Outputs:
- filtered: float32 [64, 128, 6, 6, 128], P('orb', 'brick')
- hamiltonian: float32 [64, 64], P('orb')
- margin: float32 [64, 64], P('orb')
The draws below stay inside these ranges and needn't reach their ends.
All inputs are finite; a program needn't handle non-finite values.
Results may differ from the reference program's by a relative error of at most 0.00005.
Values sent between devices are 32-bit elements; how exact they have to be, the bound alone decides.
No kernel may reach another device: no remote copies, remote signals or barrier semaphores. Data moves between devices by JAX's collectives and lax.ppermute only.
A program may use at most 64 MiB of HBM per device.

```python
import jax
import jax.numpy as jnp
from jax import lax

ORB = 64
CX = 6
CY = 6
NZ = 128
BX = 16
DEGREE = 3
BRICKS = 128
BY = 8
NX = 96
NY = 48


def draw_orbitals(key, part):
    subkeys = jax.random.split(key, 3)
    cell_shape = (BRICKS, CX, CY, NZ)
    shared = jax.random.normal(subkeys[0], (3,) + cell_shape, jnp.float32)
    mixing = jax.random.normal(subkeys[1], (ORB, 3, 1, 1, 1, 1), jnp.float32)
    private = jax.random.normal(subkeys[2], (ORB,) + cell_shape, jnp.float32)
    combined = 0.6 * private + mixing[:, 0] * shared[0] + mixing[:, 1] * shared[1] + mixing[:, 2] * shared[2]
    return jnp.clip(2.0 * combined, -24.0, 24.0)


def level_of(stream_key, shape, cuts, smallest, high):
    gain = 1.0
    for dim, shards_of in cuts:
        heights = jax.random.uniform(jax.random.fold_in(jax.random.fold_in(stream_key, 6), dim), (shards_of,), jnp.float32, smallest / len(cuts), high / len(cuts))
        gain = gain * jnp.repeat(jnp.exp(heights), shape[dim] // shards_of).reshape((-1,) + (1,) * (len(shape) - 1 - dim))
    return gain


def setup_inputs(seed: int = 0) -> dict:
    seeds = jax.random.split(jax.random.key(seed), 3)
    orbitals = draw_orbitals(jax.random.fold_in(seeds[2], 71), 0)
    potential = jnp.clip(2.0 * jax.random.uniform(seeds[1], (BRICKS, CX, CY, NZ), jnp.float32) ** level_of(seeds[1], (BRICKS, CX, CY, NZ), ((0, 128),), -0.2, 0.2), 0.0, 2.0)
    return {"orbitals": orbitals, "potential": potential}


stencil_weights = (-5369.0 / 1800.0, 12.0 / 7.0, -15.0 / 56.0, 10.0 / 189.0, -1.0 / 112.0, 2.0 / 825.0, -1.0 / 4752.0)
lower_edge = 0.0
cut_edge = 3.0
upper_edge = 13.0


def along_axis(extended, axis_number, length):
    summed = None
    for offset in range(1, 7):
        ahead_part = lax.slice_in_dim(extended, 6 + offset, 6 + offset + length, axis=axis_number)
        behind_part = lax.slice_in_dim(extended, 6 - offset, 6 - offset + length, axis=axis_number)
        weighted = stencil_weights[offset] * (ahead_part + behind_part)
        summed = weighted if summed is None else summed + weighted
    return summed


def to_grid(blocks):
    leading = blocks.shape[0]
    shaped = blocks.reshape(leading, BX, BY, CX, CY, NZ).transpose(0, 1, 3, 2, 4, 5)
    return shaped.reshape(leading, NX, NY, NZ)


def from_grid(grid):
    leading = grid.shape[0]
    shaped = grid.reshape(leading, BX, CX, BY, CY, NZ).transpose(0, 1, 3, 2, 4, 5)
    return shaped.reshape(leading, BRICKS, CX, CY, NZ)


def hamiltonian_grid(values, field_potential):
    padded = jnp.pad(values, 6)
    padded_x = padded[:, 6:6 + NY, 6:6 + NZ]
    padded_y = padded[6:6 + NX, :, 6:6 + NZ]
    padded_z = padded[6:6 + NX, 6:6 + NY, :]
    laplace = 3.0 * stencil_weights[0] * values + along_axis(padded_x, 0, NX) + along_axis(padded_y, 1, NY) + along_axis(padded_z, 2, NZ)
    return -0.5 * laplace + field_potential * values


def reference(orbitals, potential):
    grid_potential = to_grid(potential[None])[0]
    half_width = (upper_edge - cut_edge) / 2.0
    centre = (upper_edge + cut_edge) / 2.0
    sigma_first = half_width / (lower_edge - centre)
    tau_value = 2.0 / sigma_first

    def filter_one(values):
        previous = values
        current = (sigma_first / half_width) * (hamiltonian_grid(values, grid_potential) - centre * values)
        sigma_now = sigma_first
        for section in range(DEGREE - 1):
            sigma_next = 1.0 / (tau_value - sigma_now)
            following = (2.0 * sigma_next / half_width) * (hamiltonian_grid(current, grid_potential) - centre * current) - sigma_now * sigma_next * previous
            previous, current, sigma_now = current, following, sigma_next
        return current, hamiltonian_grid(current, grid_potential)

    filtered_grid, applied_grid = lax.map(filter_one, to_grid(orbitals))
    cell_count = NX * NY * NZ
    flat_filtered = filtered_grid.reshape(ORB, cell_count)
    flat_applied = applied_grid.reshape(ORB, cell_count)
    margin = jnp.einsum("ic,jc->ij", flat_filtered, flat_filtered, precision=lax.Precision.HIGHEST) / cell_count
    hamiltonian = jnp.einsum("ic,jc->ij", flat_filtered, flat_applied, precision=lax.Precision.HIGHEST) / cell_count
    return from_grid(filtered_grid), hamiltonian, margin
```

```python
import jax
import jax.numpy as jnp
from jax import lax
from jax.experimental import pallas as pl
from jax.experimental.pallas import tpu as pltpu
from jax.sharding import Mesh, PartitionSpec as P

weights = (
    -5369.0 / 1800.0,
    12.0 / 7.0,
    -15.0 / 56.0,
    10.0 / 189.0,
    -1.0 / 112.0,
    2.0 / 825.0,
    -1.0 / 4752.0,
)
lower_edge = 0.0
cut_edge = 3.0
upper_edge = 13.0
CELLS = 96 * 48 * 128

VM = pl.BlockSpec(memory_space=pltpu.VMEM)
SM = pl.BlockSpec(memory_space=pltpu.SMEM)
PARAMS = pltpu.CompilerParams(vmem_limit_bytes=32 * 1024 * 1024)
F32 = jnp.float32

HALF = jax.ShapeDtypeStruct((6, 2, 6, 8, 128), F32)
RAW = jax.ShapeDtypeStruct((1152, 128), F32)


def call(body, outs, inputs, specs=None, flops=1_000_000):
    return pl.pallas_call(
        body,
        out_shape=outs,
        in_specs=specs or [VM] * len(inputs),
        out_specs=jax.tree.map(lambda _: VM, outs),
        compiler_params=PARAMS,
        cost_estimate=pl.CostEstimate(flops=flops, bytes_accessed=2_000_000, transcendentals=0),
    )(*inputs)


def unpack_body(raw, low, high):
    for half, ref in ((0, low), (1, high)):
        for o in range(2):
            for xi in range(6):
                for yi in range(6):
                    start = half * 576 + o * 36 + xi * 6 + yi
                    ref[xi, o, yi] = raw[pl.ds(start, 8, stride=72), :]


def interior_body(alpha, shift, beta, has_previous, *refs):
    if has_previous:
        low, high, potential, previous_low, previous_high, acc_low, acc_high = refs
    else:
        low, high, potential, acc_low, acc_high = refs
    halves = (low, high)
    accs = (acc_low, acc_high)
    scaled = [-0.5 * alpha * w for w in weights]
    row = lax.broadcasted_iota(jnp.int32, (128, 128), 0)
    column = lax.broadcasted_iota(jnp.int32, (128, 128), 1)
    distance = jnp.abs(row - column)
    band = jnp.zeros((128, 128), F32)
    for k in range(1, 7):
        band = jnp.where(distance == k, F32(scaled[k]), band)
    band = jnp.where(distance == 0, F32(3.0 * scaled[0] - alpha * shift), band)
    sub = lax.broadcasted_iota(jnp.int32, (8, 128), 0)
    for x in range(12):
        here = halves[x // 6][x % 6]
        along = jnp.dot(
            here.reshape(96, 128), band, precision=lax.Precision.HIGHEST, preferred_element_type=F32
        ).reshape(2, 6, 8, 128)
        for o in range(2):
            own = [here[o, yi] for yi in range(6)]
            behind = [jnp.where(sub == 0, 0.0, pltpu.roll(v, 1, 0)) for v in own]
            ahead = [jnp.where(sub == 7, 0.0, pltpu.roll(v, 7, 0)) for v in own]
            line = behind + own + ahead
            for yi in range(6):
                start = (x // 6) * 288 + (x % 6) * 6 + yi
                local = potential[pl.ds(start, 8, stride=36), :] * F32(alpha)
                total = along[o, yi] + local * own[yi]
                for k in range(1, 7):
                    pair = line[6 + yi + k] + line[6 + yi - k]
                    if x + k < 12:
                        pair = pair + halves[(x + k) // 6][(x + k) % 6, o, yi]
                    if x - k >= 0:
                        pair = pair + halves[(x - k) // 6][(x - k) % 6, o, yi]
                    total = total + F32(scaled[k]) * pair
                if has_previous:
                    old = (previous_low, previous_high)[x // 6][x % 6, o, yi]
                    total = total - F32(beta) * old
                accs[x // 6][x % 6, o, yi] = total


def halo_terms(alpha, inside, acc_low, acc_high, before, after, emit):
    scaled = [-0.5 * alpha * w for w in weights]
    from_before = [inside[0] * F32(s) for s in scaled]
    from_after = [inside[1] * F32(s) for s in scaled]
    for o in range(2):
        for yi in range(6):
            lows = [before[j, o, yi] for j in range(6)]
            highs = [after[j, o, yi] for j in range(6)]
            for x in range(6):
                total = acc_low[x, o, yi]
                for k in range(x + 1, 7):
                    total = total + from_before[k] * lows[6 + x - k]
                emit(0, x, o, yi, total)
                total = acc_high[5 - x, o, yi]
                for k in range(x + 1, 7):
                    total = total + from_after[k] * highs[k - x - 1]
                emit(1, 5 - x, o, yi, total)


def edge_body(alpha, inside, acc_low, acc_high, before, after, out_low, out_high):
    outs = (out_low, out_high)

    def emit(half, x, o, yi, value):
        outs[half][x, o, yi] = value

    halo_terms(alpha, inside, acc_low, acc_high, before, after, emit)


def edge_both_body(alpha, inside, acc_low, acc_high, before, after, out_low, out_high, raw):
    outs = (out_low, out_high)

    def emit(half, x, o, yi, value):
        outs[half][x, o, yi] = value
        raw[pl.ds(half * 576 + o * 36 + x * 6 + yi, 8, stride=72), :] = value

    halo_terms(alpha, inside, acc_low, acc_high, before, after, emit)


def edge_raw_body(alpha, inside, acc_low, acc_high, before, after, raw):
    def emit(half, x, o, yi, value):
        raw[pl.ds(half * 576 + o * 36 + x * 6 + yi, 8, stride=72), :] = value

    halo_terms(alpha, inside, acc_low, acc_high, before, after, emit)


def gram_body(mine, other, applied, copies):
    total = jnp.zeros((64, 64), F32)
    for r in range(36):
        rows = pl.ds(r, 32, stride=36)
        own = mine[rows, :]
        left = jnp.concatenate([own, applied[rows, :]], axis=0)
        right = jnp.concatenate([own, other[rows, :]], axis=0)
        total = total + lax.dot_general(
            left,
            right,
            (((1,), (1,)), ((), ())),
            precision=lax.Precision.HIGHEST,
            preferred_element_type=F32,
        )
    packed = jnp.concatenate([total[:32], total[32:]], axis=1)
    for n in range(16):
        copies[n] = packed


def sum_body(parts, copies):
    total = parts[0]
    for n in range(1, 16):
        total = total + parts[n]
    for n in range(8):
        copies[n] = total


def finish_body(side, parts, energy, margin):
    total = parts[0]
    for n in range(1, 8):
        total = total + parts[n]
    total = total * F32(1.0 / CELLS)
    swapped = jnp.concatenate(
        [total[:, 32:64], total[:, 0:32], total[:, 96:128], total[:, 64:96]], axis=1
    )
    total = jnp.where(side[0] == 0, total, swapped)
    margin[...] = total[:, :64]
    energy[...] = total[:, 64:]


SLAB = ("xl", "y", "core")


def local(orbitals, potential):
    position = lax.axis_index("z")
    inside = jnp.stack([position > 0, position < 7]).astype(F32)
    side = lax.axis_index("xh").astype(jnp.int32).reshape(1)
    field = lax.all_gather(potential.reshape(36, 128), SLAB, axis=0, tiled=True)
    raw = lax.all_to_all(
        orbitals.reshape(16, 72, 128), SLAB, split_axis=0, concat_axis=0, tiled=True
    ).reshape(1152, 128)
    current = call(unpack_body, [HALF, HALF], [raw])
    up = [(i, (i + 1) % 8) for i in range(8)]
    down = [(i, (i + 7) % 8) for i in range(8)]

    def hamiltonian_part(alpha, shift, beta, values, previous, body, outs):
        before = lax.ppermute(values[1], "z", up)
        after = lax.ppermute(values[0], "z", down)

        def interior(*refs):
            interior_body(alpha, shift, beta, previous is not None, *refs)

        accs = call(interior, [HALF, HALF], [*values, field] + list(previous or []), flops=20_000_000)

        def edge(*refs):
            body(alpha, *refs)

        return call(edge, outs, [inside, *accs, before, after], [SM] + [VM] * 4)

    half_width = (upper_edge - cut_edge) / 2.0
    centre = (upper_edge + cut_edge) / 2.0
    sigma_first = half_width / (lower_edge - centre)
    tau_value = 2.0 / sigma_first
    previous = current
    current = hamiltonian_part(
        sigma_first / half_width, centre, 0.0, current, None, edge_body, [HALF, HALF]
    )
    sigma_second = 1.0 / (tau_value - sigma_first)
    previous, current = current, hamiltonian_part(
        2.0 * sigma_second / half_width,
        centre,
        sigma_first * sigma_second,
        current,
        previous,
        edge_body,
        [HALF, HALF],
    )
    sigma_third = 1.0 / (tau_value - sigma_second)
    low, high, filtered_raw = hamiltonian_part(
        2.0 * sigma_third / half_width,
        centre,
        sigma_second * sigma_third,
        current,
        previous,
        edge_both_body,
        [HALF, HALF, RAW],
    )

    def to_bricks(values):
        return lax.all_to_all(
            values.reshape(16, 72, 128), SLAB, split_axis=0, concat_axis=0, tiled=True
        ).reshape(1152, 128)

    filtered = to_bricks(filtered_raw)
    other = lax.ppermute(filtered, "xh", [(0, 1), (1, 0)])
    applied_raw = hamiltonian_part(1.0, 0.0, 0.0, [low, high], None, edge_raw_body, RAW)
    applied = to_bricks(applied_raw)
    copies = call(gram_body, jax.ShapeDtypeStruct((16, 32, 128), F32), [filtered, other, applied])
    parts = lax.all_to_all(copies, SLAB, split_axis=0, concat_axis=0, tiled=True)
    copies = call(sum_body, jax.ShapeDtypeStruct((8, 32, 128), F32), [parts])
    parts = lax.all_to_all(copies, "z", split_axis=0, concat_axis=0, tiled=True)
    energy, margin = call(
        finish_body,
        [jax.ShapeDtypeStruct((32, 64), F32)] * 2,
        [side, parts],
        [SM, VM],
    )
    return filtered.reshape(32, 1, 6, 6, 128), energy, margin


def solution(mesh):
    fine = Mesh(mesh.devices.reshape(8, 2, 4, 2, 2), ("z", "xl", "y", "core", "xh"))
    brick = ("z", "xl", "y", "core")
    return jax.shard_map(
        local,
        mesh=fine,
        in_specs=(P("xh", brick, None, None, None), P(brick, None, None, None)),
        out_specs=(P("xh", brick, None, None, None), P("xh", None), P("xh", None)),
        check_vma=False,
    )
```

```python
import jax
import jax.numpy as jnp
from jax import lax
from jax.experimental import pallas as pl
from jax.experimental.pallas import tpu as pltpu
from jax.sharding import Mesh, PartitionSpec as P

weights = (
    -5369.0 / 1800.0,
    12.0 / 7.0,
    -15.0 / 56.0,
    10.0 / 189.0,
    -1.0 / 112.0,
    2.0 / 825.0,
    -1.0 / 4752.0,
)
lower_edge = 0.0
cut_edge = 3.0
upper_edge = 13.0
CELLS = 96 * 48 * 128

VM = pl.BlockSpec(memory_space=pltpu.VMEM)
SM = pl.BlockSpec(memory_space=pltpu.SMEM)
PARAMS = pltpu.CompilerParams(vmem_limit_bytes=32 * 1024 * 1024)
F32 = jnp.float32

HALF = jax.ShapeDtypeStruct((6, 12, 8, 128), F32)
RAW = jax.ShapeDtypeStruct((1152, 128), F32)
WIDE = jax.ShapeDtypeStruct((15, 12, 8, 128), F32)


def call(body, outs, inputs, specs=None, out_specs=None, scratch=(), flops=1_000_000):
    return pl.pallas_call(
        body,
        out_shape=outs,
        in_specs=specs or [VM] * len(inputs),
        out_specs=out_specs or jax.tree.map(lambda _: VM, outs),
        scratch_shapes=scratch,
        compiler_params=PARAMS,
        cost_estimate=pl.CostEstimate(flops=flops, bytes_accessed=2_000_000, transcendentals=0),
    )(*inputs)


def unpack_body(raw, to_up, to_down):
    for half in range(2):
        for xi in range(6):
            for yi in range(6):
                for o in range(2):
                    rows = raw[pl.ds(half * 896 + o * 36 + xi * 6 + yi, 8, stride=112), :]
                    to_up[half * 6 + xi, o * 6 + yi] = rows
                    to_down[half * 6 + xi, o * 6 + yi] = rows
                rows = raw[pl.ds(half * 896 + 72 + xi * 6 + yi, 8, stride=112), :]
                (to_down, to_up)[half][12 + xi // 2, (xi % 2) * 6 + yi] = rows


class Step:
    def __init__(self, alpha, shift):
        self.alpha = alpha
        self.scaled = [-0.5 * alpha * w for w in weights]
        row = lax.broadcasted_iota(jnp.int32, (128, 128), 0)
        column = lax.broadcasted_iota(jnp.int32, (128, 128), 1)
        distance = jnp.abs(row - column)
        band = jnp.zeros((128, 128), F32)
        for k in range(1, 7):
            band = jnp.where(distance == k, F32(self.scaled[k]), band)
        self.band = jnp.where(distance == 0, F32(3.0 * self.scaled[0] - alpha * shift), band)
        self.sub = lax.broadcasted_iota(jnp.int32, (8, 128), 0)

    def plane(self, x, layer, local, emit):
        ref, index = layer(x)
        here = ref[index]
        along = jnp.dot(
            here.reshape(96, 128), self.band, precision=lax.Precision.HIGHEST, preferred_element_type=F32
        ).reshape(12, 8, 128)
        near = [(k, [p for p in (layer(x + k), layer(x - k)) if p is not None]) for k in range(1, 7)]
        for o in range(2):
            own = [ref[index, o * 6 + yi] for yi in range(6)]
            behind = [jnp.where(self.sub == 0, 0.0, pltpu.roll(v, 1, 0)) for v in own]
            ahead = [jnp.where(self.sub == 7, 0.0, pltpu.roll(v, 7, 0)) for v in own]
            line = behind + own + ahead
            for yi in range(6):
                n = o * 6 + yi
                total = along[n] + local(yi) * F32(self.alpha) * own[yi]
                for k, planes in near:
                    pair = line[6 + yi + k] + line[6 + yi - k]
                    for other, place in planes:
                        pair = pair + other[place, n]
                    total = total + F32(self.scaled[k]) * pair
                emit(n, total)


def field_of(to_up, to_down):
    def rows(x, yi):
        source = to_down if x < 6 else to_up
        return source[12 + (x % 6) // 2, (x % 2) * 6 + yi]

    return rows


def first_body(alpha, shift, to_up, to_down, acc):
    step = Step(alpha, shift)
    field = field_of(to_up, to_down)
    for x in range(12):

        def emit(n, value, x=x):
            acc[x, n] = value

        step.plane(
            x,
            lambda i: (to_up, i) if 0 <= i < 12 else None,
            lambda yi, x=x: field(x, yi),
            emit,
        )


def two_steps_body(first, second, inside, to_up, to_down, before, after, acc, y1_low, y1_high, y2_low, y2_high, wide):
    step = Step(first[0], first[1])
    field = field_of(to_up, to_down)
    mask = (inside[0], inside[1])
    terms_before = [mask[0] * F32(s) for s in step.scaled]
    terms_after = [mask[1] * F32(s) for s in step.scaled]
    for n in range(12):
        lows = [before[6 + j, n] for j in range(6)]
        highs = [after[j, n] for j in range(6)]
        for x in range(6):
            total = acc[x, n]
            for k in range(x + 1, 7):
                total = total + terms_before[k] * lows[6 + x - k]
            wide[6 + x, n] = total
            y1_low[x, n] = total
            total = acc[11 - x, n]
            for k in range(x + 1, 7):
                total = total + terms_after[k] * highs[k - x - 1]
            wide[17 - x, n] = total
            y1_high[5 - x, n] = total

    def layer(i):
        if i < 0:
            return before, 12 + i
        return (to_up, i) if i < 12 else (after, i - 12)

    for j in range(6):
        for x, source, side in ((j - 6, before, 0), (12 + j, after, 1)):

            def emit(n, value, x=x, side=side):
                wide[6 + x, n] = value * mask[side]

            step.plane(
                x,
                layer,
                lambda yi, j=j, source=source: source[12 + j // 2, (j % 2) * 6 + yi],
                emit,
            )
    step = Step(second[0], second[1])
    beta = second[2]
    for x in range(12):

        def emit(n, value, x=x):
            (y2_low, y2_high)[x // 6][x % 6, n] = value - F32(beta) * to_up[x, n]

        step.plane(x, lambda i: (wide, 6 + i), lambda yi, x=x: field(x, yi), emit)


def interior_body(alpha, shift, beta, low, high, to_up, to_down, *refs):
    if len(refs) == 2:
        acc_low, acc_high = refs
    else:
        previous_low, previous_high, acc_low, acc_high = refs
    step = Step(alpha, shift)
    field = field_of(to_up, to_down)
    for x in range(12):

        def emit(n, value, x=x):
            if len(refs) == 4:
                value = value - F32(beta) * (previous_low, previous_high)[x // 6][x % 6, n]
            (acc_low, acc_high)[x // 6][x % 6, n] = value

        step.plane(
            x,
            lambda i: ((low, high)[i // 6], i % 6) if 0 <= i < 12 else None,
            lambda yi, x=x: field(x, yi),
            emit,
        )


def halo_terms(alpha, inside, acc_low, acc_high, before, after, emit):
    scaled = [-0.5 * alpha * w for w in weights]
    terms_before = [inside[0] * F32(s) for s in scaled]
    terms_after = [inside[1] * F32(s) for s in scaled]
    for n in range(12):
        lows = [before[j, n] for j in range(6)]
        highs = [after[j, n] for j in range(6)]
        for x in range(6):
            total = acc_low[x, n]
            for k in range(x + 1, 7):
                total = total + terms_before[k] * lows[6 + x - k]
            emit(0, x, n, total)
            total = acc_high[5 - x, n]
            for k in range(x + 1, 7):
                total = total + terms_after[k] * highs[k - x - 1]
            emit(1, 5 - x, n, total)


def brick_rows(half, x, n):
    return pl.ds(half * 576 + (n // 6) * 36 + x * 6 + n % 6, 8, stride=72)


def edge_both_body(alpha, inside, acc_low, acc_high, before, after, out_low, out_high, raw):
    outs = (out_low, out_high)

    def emit(half, x, n, value):
        outs[half][x, n] = value
        raw[brick_rows(half, x, n), :] = value

    halo_terms(alpha, inside, acc_low, acc_high, before, after, emit)


def edge_raw_body(alpha, inside, acc_low, acc_high, before, after, raw):
    def emit(half, x, n, value):
        raw[brick_rows(half, x, n), :] = value

    halo_terms(alpha, inside, acc_low, acc_high, before, after, emit)


def gram_body(mine, other, applied, copies, out, sem):
    write = pltpu.make_async_copy(mine, out, sem)
    write.start()
    total = jnp.zeros((64, 64), F32)
    for r in range(36):
        rows = pl.ds(r, 32, stride=36)
        own = mine[rows, :]
        left = jnp.concatenate([own, applied[rows, :]], axis=0)
        right = jnp.concatenate([own, other[rows, :]], axis=0)
        total = total + lax.dot_general(
            left,
            right,
            (((1,), (1,)), ((), ())),
            precision=lax.Precision.HIGHEST,
            preferred_element_type=F32,
        )
    packed = jnp.concatenate([total[:32], total[32:]], axis=1)
    for n in range(16):
        copies[n] = packed
    write.wait()


def sum_body(parts, copies):
    total = parts[0]
    for n in range(1, 16):
        total = total + parts[n]
    for n in range(8):
        copies[n] = total


def finish_body(side, parts, energy, margin):
    total = parts[0]
    for n in range(1, 8):
        total = total + parts[n]
    total = total * F32(1.0 / CELLS)
    swapped = jnp.concatenate(
        [total[:, 32:64], total[:, 0:32], total[:, 96:128], total[:, 64:96]], axis=1
    )
    total = jnp.where(side[0] == 0, total, swapped)
    margin[...] = total[:, :64]
    energy[...] = total[:, 64:]


SLAB = ("xl", "y", "core")
UP = [(i, (i + 1) % 8) for i in range(8)]
DOWN = [(i, (i + 7) % 8) for i in range(8)]


def to_slabs(values):
    return lax.all_to_all(values, SLAB, split_axis=0, concat_axis=0, tiled=True)


def local(orbitals, potential):
    position = lax.axis_index("z")
    inside = jnp.stack([position > 0, position < 7]).astype(F32)
    side = lax.axis_index("xh").astype(jnp.int32).reshape(1)

    half_width = (upper_edge - cut_edge) / 2.0
    centre = (upper_edge + cut_edge) / 2.0
    sigma_first = half_width / (lower_edge - centre)
    tau_value = 2.0 / sigma_first
    sigma_second = 1.0 / (tau_value - sigma_first)
    sigma_third = 1.0 / (tau_value - sigma_second)
    first = (sigma_first / half_width, centre, 0.0)
    second = (2.0 * sigma_second / half_width, centre, sigma_first * sigma_second)
    third = (2.0 * sigma_third / half_width, centre, sigma_second * sigma_third)

    field = jnp.pad(potential.reshape(1, 36, 128), ((0, 0), (0, 4), (0, 0)))
    field = jnp.broadcast_to(field, (16, 40, 128))
    joined = jnp.concatenate([orbitals.reshape(16, 72, 128), field], axis=1)
    raw = to_slabs(joined).reshape(1792, 128)
    packed = call(unpack_body, [WIDE, WIDE], [raw])

    before = lax.ppermute(packed[0], "z", UP)
    after = lax.ppermute(packed[1], "z", DOWN)

    def first_part(*refs):
        first_body(first[0], first[1], *refs)

    acc = call(first_part, jax.ShapeDtypeStruct((12, 12, 8, 128), F32), packed, flops=400_000_000)

    def two_steps(*refs):
        two_steps_body(first, second, *refs)

    y1_low, y1_high, y2_low, y2_high = call(
        two_steps,
        [HALF] * 4,
        [inside, *packed, before, after, acc],
        [SM] + [VM] * 5,
        scratch=[pltpu.VMEM((24, 12, 8, 128), F32)],
    )

    def one_step(numbers, values, previous, body, outs):
        alpha, shift, beta = numbers
        before = lax.ppermute(values[1], "z", UP)
        after = lax.ppermute(values[0], "z", DOWN)

        def interior(*refs):
            interior_body(alpha, shift, beta, *refs)

        accs = call(interior, [HALF, HALF], [*values, *packed, *previous], flops=400_000_000)

        def edge(*refs):
            body(alpha, *refs)

        return call(edge, outs, [inside, *accs, before, after], [SM] + [VM] * 4)

    low, high, filtered_raw = one_step(
        third, (y2_low, y2_high), (y1_low, y1_high), edge_both_body, [HALF, HALF, RAW]
    )
    filtered = to_slabs(filtered_raw.reshape(16, 72, 128)).reshape(1152, 128)
    other = lax.ppermute(filtered, "xh", [(0, 1), (1, 0)])
    applied_raw = one_step((1.0, 0.0, 0.0), (low, high), (), edge_raw_body, RAW)
    applied = to_slabs(applied_raw.reshape(16, 72, 128)).reshape(1152, 128)
    copies, result = call(
        gram_body,
        [jax.ShapeDtypeStruct((16, 32, 128), F32), RAW],
        [filtered, other, applied],
        out_specs=[VM, pl.BlockSpec(memory_space=pl.ANY)],
        scratch=[pltpu.SemaphoreType.DMA],
    )
    parts = to_slabs(copies)
    copies = call(sum_body, jax.ShapeDtypeStruct((8, 32, 128), F32), [parts])
    parts = lax.all_to_all(copies, "z", split_axis=0, concat_axis=0, tiled=True)
    energy, margin = call(
        finish_body,
        [jax.ShapeDtypeStruct((32, 64), F32)] * 2,
        [side, parts],
        [SM, VM],
    )
    return result.reshape(32, 1, 6, 6, 128), energy, margin


def solution(mesh):
    fine = Mesh(mesh.devices.reshape(8, 2, 4, 2, 2), ("z", "xl", "y", "core", "xh"))
    brick = ("z", "xl", "y", "core")
    return jax.shard_map(
        local,
        mesh=fine,
        in_specs=(P("xh", brick, None, None, None), P(brick, None, None, None)),
        out_specs=(P("xh", brick, None, None, None), P("xh", None), P("xh", None)),
        check_vma=False,
    )
```

```python
import jax
import jax.numpy as jnp
from jax import lax
from jax.experimental import pallas as pl
from jax.experimental.pallas import tpu as pltpu
from jax.sharding import Mesh, PartitionSpec as P

weights = (
    -5369.0 / 1800.0,
    12.0 / 7.0,
    -15.0 / 56.0,
    10.0 / 189.0,
    -1.0 / 112.0,
    2.0 / 825.0,
    -1.0 / 4752.0,
)
lower_edge = 0.0
cut_edge = 3.0
upper_edge = 13.0
CELLS = 96 * 48 * 128

VM = pl.BlockSpec(memory_space=pltpu.VMEM)
SM = pl.BlockSpec(memory_space=pltpu.SMEM)
PARAMS = pltpu.CompilerParams(vmem_limit_bytes=32 * 1024 * 1024)
F32 = jnp.float32

HALF = jax.ShapeDtypeStruct((6, 12, 8, 128), F32)
RAW = jax.ShapeDtypeStruct((1152, 128), F32)
SLABF = jax.ShapeDtypeStruct((12, 12, 8, 128), F32)


def call(body, outs, inputs, specs=None, out_specs=None, scratch=(), flops=1_000_000):
    return pl.pallas_call(
        body,
        out_shape=outs,
        in_specs=specs or [VM] * len(inputs),
        out_specs=out_specs or jax.tree.map(lambda _: VM, outs),
        scratch_shapes=scratch,
        compiler_params=PARAMS,
        cost_estimate=pl.CostEstimate(flops=flops, bytes_accessed=2_000_000, transcendentals=0),
    )(*inputs)


def unpack_body(raw, planes):
    for half in range(2):
        for xi in range(6):
            for n in range(12):
                planes[half * 6 + xi, n] = raw[brick_rows(half, xi, n), :]


def brick_rows(half, x, n):
    return pl.ds(half * 576 + (n // 6) * 36 + x * 6 + n % 6, 8, stride=72)


def field_rows(field, x, yi):
    if 0 <= x < 12:
        return field[pl.ds((x // 6) * 576 + (x % 6) * 6 + yi, 8, stride=72), :]
    half = 0 if x < 0 else 1
    return field[pl.ds(half * 576 + 36 + (x % 6) * 6 + yi, 8, stride=72), :]


class Step:
    def __init__(self, alpha, shift):
        self.alpha = alpha
        self.scaled = [-0.5 * alpha * w for w in weights]
        row = lax.broadcasted_iota(jnp.int32, (128, 128), 0)
        column = lax.broadcasted_iota(jnp.int32, (128, 128), 1)
        distance = jnp.abs(row - column)
        band = jnp.zeros((128, 128), F32)
        for k in range(1, 7):
            band = jnp.where(distance == k, F32(self.scaled[k]), band)
        self.band = jnp.where(distance == 0, F32(3.0 * self.scaled[0] - alpha * shift), band)
        self.sub = lax.broadcasted_iota(jnp.int32, (8, 128), 0)

    def plane(self, x, layer, local, emit):
        ref, index = layer(x)
        here = ref[index]
        along = jnp.dot(
            here.reshape(96, 128), self.band, precision=lax.Precision.HIGHEST, preferred_element_type=F32
        ).reshape(12, 8, 128)
        near = [(k, [p for p in (layer(x + k), layer(x - k)) if p is not None]) for k in range(1, 7)]
        for o in range(2):
            own = [ref[index, o * 6 + yi] for yi in range(6)]
            behind = [jnp.where(self.sub == 0, 0.0, pltpu.roll(v, 1, 0)) for v in own]
            ahead = [jnp.where(self.sub == 7, 0.0, pltpu.roll(v, 7, 0)) for v in own]
            line = behind + own + ahead
            for yi in range(6):
                n = o * 6 + yi
                total = along[n] + local(yi) * F32(self.alpha) * own[yi]
                for k, planes in near:
                    pair = line[6 + yi + k] + line[6 + yi - k]
                    for other, place in planes:
                        pair = pair + other[place, n]
                    total = total + F32(self.scaled[k]) * pair
                emit(n, total)


def first_body(alpha, shift, planes, field, acc):
    step = Step(alpha, shift)
    for x in range(12):

        def emit(n, value, x=x):
            acc[x, n] = value

        step.plane(
            x,
            lambda i: (planes, i) if 0 <= i < 12 else None,
            lambda yi, x=x: field_rows(field, x, yi),
            emit,
        )


def two_steps_body(first, second, inside, planes, field, before, after, acc, y1_low, y1_high, y2_low, y2_high, wide):
    step = Step(first[0], first[1])
    mask = (inside[0], inside[1])
    terms_before = [mask[0] * F32(s) for s in step.scaled]
    terms_after = [mask[1] * F32(s) for s in step.scaled]
    for n in range(12):
        lows = [before[6 + j, n] for j in range(6)]
        highs = [after[j, n] for j in range(6)]
        for x in range(6):
            total = acc[x, n]
            for k in range(x + 1, 7):
                total = total + terms_before[k] * lows[6 + x - k]
            wide[6 + x, n] = total
            y1_low[x, n] = total
            total = acc[11 - x, n]
            for k in range(x + 1, 7):
                total = total + terms_after[k] * highs[k - x - 1]
            wide[17 - x, n] = total
            y1_high[5 - x, n] = total

    def layer(i):
        if i < 0:
            return before, 12 + i
        return (planes, i) if i < 12 else (after, i - 12)

    for j in range(6):
        for x, side in ((j - 6, 0), (12 + j, 1)):

            def emit(n, value, x=x, side=side):
                wide[6 + x, n] = value * mask[side]

            step.plane(
                x,
                layer,
                lambda yi, x=x: field_rows(field, x, yi),
                emit,
            )
    step = Step(second[0], second[1])
    beta = second[2]
    for x in range(12):

        def emit(n, value, x=x):
            (y2_low, y2_high)[x // 6][x % 6, n] = value - F32(beta) * planes[x, n]

        step.plane(x, lambda i: (wide, 6 + i), lambda yi, x=x: field_rows(field, x, yi), emit)


def interior_body(alpha, shift, beta, low, high, field, *refs):
    if len(refs) == 2:
        acc_low, acc_high = refs
    else:
        previous_low, previous_high, acc_low, acc_high = refs
    step = Step(alpha, shift)
    for x in range(12):

        def emit(n, value, x=x):
            if len(refs) == 4:
                value = value - F32(beta) * (previous_low, previous_high)[x // 6][x % 6, n]
            (acc_low, acc_high)[x // 6][x % 6, n] = value

        step.plane(
            x,
            lambda i: ((low, high)[i // 6], i % 6) if 0 <= i < 12 else None,
            lambda yi, x=x: field_rows(field, x, yi),
            emit,
        )


def halo_terms(alpha, inside, acc_low, acc_high, before, after, emit):
    scaled = [-0.5 * alpha * w for w in weights]
    terms_before = [inside[0] * F32(s) for s in scaled]
    terms_after = [inside[1] * F32(s) for s in scaled]
    for n in range(12):
        lows = [before[j, n] for j in range(6)]
        highs = [after[j, n] for j in range(6)]
        for x in range(6):
            total = acc_low[x, n]
            for k in range(x + 1, 7):
                total = total + terms_before[k] * lows[6 + x - k]
            emit(0, x, n, total)
            total = acc_high[5 - x, n]
            for k in range(x + 1, 7):
                total = total + terms_after[k] * highs[k - x - 1]
            emit(1, 5 - x, n, total)


def edge_both_body(alpha, inside, acc_low, acc_high, before, after, out_low, out_high, raw):
    outs = (out_low, out_high)

    def emit(half, x, n, value):
        outs[half][x, n] = value
        raw[brick_rows(half, x, n), :] = value

    halo_terms(alpha, inside, acc_low, acc_high, before, after, emit)


def edge_raw_body(alpha, inside, acc_low, acc_high, before, after, raw):
    def emit(half, x, n, value):
        raw[brick_rows(half, x, n), :] = value

    halo_terms(alpha, inside, acc_low, acc_high, before, after, emit)


def gram_body(mine, other, applied, copies, out, sem):
    write = pltpu.make_async_copy(mine, out, sem)
    write.start()
    total = jnp.zeros((64, 64), F32)
    for r in range(36):
        rows = pl.ds(r, 32, stride=36)
        own = mine[rows, :]
        left = jnp.concatenate([own, applied[rows, :]], axis=0)
        right = jnp.concatenate([own, other[rows, :]], axis=0)
        total = total + lax.dot_general(
            left,
            right,
            (((1,), (1,)), ((), ())),
            precision=lax.Precision.HIGHEST,
            preferred_element_type=F32,
        )
    packed = jnp.concatenate([total[:32], total[32:]], axis=1)
    for n in range(16):
        copies[n] = packed
    write.wait()


def sum_body(parts, copies):
    total = parts[0]
    for n in range(1, 16):
        total = total + parts[n]
    for n in range(8):
        copies[n] = total


def finish_body(side, parts, energy, margin):
    total = parts[0]
    for n in range(1, 8):
        total = total + parts[n]
    total = total * F32(1.0 / CELLS)
    swapped = jnp.concatenate(
        [total[:, 32:64], total[:, 0:32], total[:, 96:128], total[:, 64:96]], axis=1
    )
    total = jnp.where(side[0] == 0, total, swapped)
    margin[...] = total[:, :64]
    energy[...] = total[:, 64:]


SLAB = ("xl", "y", "core")
UP = [(i, (i + 1) % 8) for i in range(8)]
DOWN = [(i, (i + 7) % 8) for i in range(8)]


def to_slabs(values):
    return lax.all_to_all(values, SLAB, split_axis=0, concat_axis=0, tiled=True)


def local(orbitals, potential):
    position = lax.axis_index("z")
    inside = jnp.stack([position > 0, position < 7]).astype(F32)
    side = lax.axis_index("xh").astype(jnp.int32).reshape(1)

    half_width = (upper_edge - cut_edge) / 2.0
    centre = (upper_edge + cut_edge) / 2.0
    sigma_first = half_width / (lower_edge - centre)
    tau_value = 2.0 / sigma_first
    sigma_second = 1.0 / (tau_value - sigma_first)
    sigma_third = 1.0 / (tau_value - sigma_second)
    first = (sigma_first / half_width, centre, 0.0)
    second = (2.0 * sigma_second / half_width, centre, sigma_first * sigma_second)
    third = (2.0 * sigma_third / half_width, centre, sigma_second * sigma_third)

    own_field = potential.reshape(36, 128)
    across = [(2 * i + 1, (2 * i + 2) % 16) for i in range(8)] + [(2 * i, (2 * i + 15) % 16) for i in range(8)]
    next_field = lax.ppermute(own_field, ("z", "xl"), across)
    raw = to_slabs(orbitals.reshape(16, 72, 128)).reshape(1152, 128)
    planes = call(unpack_body, SLABF, [raw])
    before = lax.ppermute(planes, "z", UP)
    after = lax.ppermute(planes, "z", DOWN)
    field = jnp.broadcast_to(jnp.concatenate([own_field, next_field])[None], (16, 72, 128))
    field, planes = lax.optimization_barrier((field, planes))
    field = to_slabs(field).reshape(1152, 128)

    def first_part(*refs):
        first_body(first[0], first[1], *refs)

    acc = call(first_part, SLABF, [planes, field], flops=400_000_000)

    def two_steps(*refs):
        two_steps_body(first, second, *refs)

    y1_low, y1_high, y2_low, y2_high = call(
        two_steps,
        [HALF] * 4,
        [inside, planes, field, before, after, acc],
        [SM] + [VM] * 5,
        scratch=[pltpu.VMEM((24, 12, 8, 128), F32)],
    )

    def exchange(values):
        return lax.ppermute(values[1], "z", UP), lax.ppermute(values[0], "z", DOWN)

    def interior_of(numbers, values, previous):
        def interior(*refs):
            interior_body(*numbers, *refs)

        return call(interior, [HALF, HALF], [*values, field, *previous], flops=400_000_000)

    def finish(numbers, accs, halos, body, outs):
        def edge(*refs):
            body(numbers[0], *refs)

        return call(edge, outs, [inside, *accs, *halos], [SM] + [VM] * 4)

    halos = exchange((y2_low, y2_high))
    accs = interior_of(third, (y2_low, y2_high), (y1_low, y1_high))
    low, high, filtered_raw = finish(third, accs, halos, edge_both_body, [HALF, HALF, RAW])
    filtered = to_slabs(filtered_raw.reshape(16, 72, 128)).reshape(1152, 128)
    halos = exchange((low, high))
    accs = interior_of((1.0, 0.0, 0.0), (low, high), ())
    filtered, accs = lax.optimization_barrier((filtered, accs))
    other = lax.ppermute(filtered, "xh", [(0, 1), (1, 0)])
    applied_raw = finish((1.0, 0.0, 0.0), accs, halos, edge_raw_body, RAW)
    applied = to_slabs(applied_raw.reshape(16, 72, 128)).reshape(1152, 128)
    copies, result = call(
        gram_body,
        [jax.ShapeDtypeStruct((16, 32, 128), F32), RAW],
        [filtered, other, applied],
        out_specs=[VM, pl.BlockSpec(memory_space=pl.ANY)],
        scratch=[pltpu.SemaphoreType.DMA],
    )
    parts = to_slabs(copies)
    copies = call(sum_body, jax.ShapeDtypeStruct((8, 32, 128), F32), [parts])
    parts = lax.all_to_all(copies, "z", split_axis=0, concat_axis=0, tiled=True)
    energy, margin = call(
        finish_body,
        [jax.ShapeDtypeStruct((32, 64), F32)] * 2,
        [side, parts],
        [SM, VM],
    )
    return result.reshape(32, 1, 6, 6, 128), energy, margin


def solution(mesh):
    fine = Mesh(mesh.devices.reshape(8, 2, 4, 2, 2), ("z", "xl", "y", "core", "xh"))
    brick = ("z", "xl", "y", "core")
    return jax.shard_map(
        local,
        mesh=fine,
        in_specs=(P("xh", brick, None, None, None), P(brick, None, None, None)),
        out_specs=(P("xh", brick, None, None, None), P("xh", None), P("xh", None)),
        check_vma=False,
    )
```

```python
import jax
import jax.numpy as jnp
from jax import lax
from jax.experimental import pallas as pl
from jax.experimental.pallas import tpu as pltpu
from jax.sharding import Mesh, PartitionSpec as P

weights = (
    -5369.0 / 1800.0,
    12.0 / 7.0,
    -15.0 / 56.0,
    10.0 / 189.0,
    -1.0 / 112.0,
    2.0 / 825.0,
    -1.0 / 4752.0,
)
lower_edge = 0.0
cut_edge = 3.0
upper_edge = 13.0
CELLS = 96 * 48 * 128

VM = pl.BlockSpec(memory_space=pltpu.VMEM)
SM = pl.BlockSpec(memory_space=pltpu.SMEM)
PARAMS = pltpu.CompilerParams(vmem_limit_bytes=32 * 1024 * 1024)
F32 = jnp.float32

HALF = jax.ShapeDtypeStruct((6, 12, 8, 128), F32)
FULL = jax.ShapeDtypeStruct((12, 12, 8, 128), F32)


def call(body, outs, inputs, specs=None, out_specs=None, scratch=(), flops=1_000_000):
    return pl.pallas_call(
        body,
        out_shape=outs,
        in_specs=specs or [VM] * len(inputs),
        out_specs=out_specs or jax.tree.map(lambda _: VM, outs),
        scratch_shapes=scratch,
        compiler_params=PARAMS,
        cost_estimate=pl.CostEstimate(flops=flops, bytes_accessed=2_000_000, transcendentals=0),
    )(*inputs)


def assemble_body(place, keep, received, own_field, other_field, full, low, high, field):
    first = place[0] == 0
    for xi in range(6):
        for yi in range(6):
            r = xi * 6 + yi
            for g in range(2):
                rows = pl.ds(g * 288 + r, 8, stride=36)
                a = keep[rows, :]
                b = received[rows, :]
                n = yi * 2 + g
                left = jnp.where(first, a, b)
                right = jnp.where(first, b, a)
                full[xi, n] = left
                low[xi, n] = left
                full[6 + xi, n] = right
                high[xi, n] = right
            a = jnp.broadcast_to(own_field[pl.ds(r, 1), :], (8, 128))
            b = jnp.broadcast_to(other_field[pl.ds(r, 1), :], (8, 128))
            field[xi, yi] = jnp.where(first, a, b)
            field[6 + xi, yi] = jnp.where(first, b, a)


def interior_body(alpha, shift, beta, full, field, *refs):
    acc = refs[-1]
    scaled = [-0.5 * alpha * w for w in weights]
    row = lax.broadcasted_iota(jnp.int32, (128, 128), 0)
    column = lax.broadcasted_iota(jnp.int32, (128, 128), 1)
    distance = jnp.abs(row - column)
    band = jnp.zeros((128, 128), F32)
    for k in range(1, 7):
        band = jnp.where(distance == k, F32(scaled[k]), band)
    band = jnp.where(distance == 0, F32(3.0 * scaled[0] - alpha * shift), band)
    for x in range(12):
        along = jnp.dot(
            full[x].reshape(96, 128), band, precision=lax.Precision.HIGHEST, preferred_element_type=F32
        ).reshape(12, 8, 128)
        for g in range(2):
            line = [full[x, yi * 2 + g] for yi in range(6)]
            for yi in range(6):
                n = yi * 2 + g
                total = along[n] + field[x, yi] * F32(alpha) * line[yi]
                for k in range(1, 7):
                    near = [line[yi + s] for s in (k, -k) if 0 <= yi + s < 6]
                    near += [full[x + s, n] for s in (k, -k) if 0 <= x + s < 12]
                    if near:
                        pair = near[0]
                        for v in near[1:]:
                            pair = pair + v
                        total = total + F32(scaled[k]) * pair
                if len(refs) == 2:
                    total = total - F32(beta) * refs[0][x, n]
                acc[x, n] = total


def edge_body(alpha, inside, acc, before_x, after_x, before_y, after_y, full, *halves):
    scaled = [-0.5 * alpha * w for w in weights]
    from_x = [[inside[i] * F32(s) for s in scaled] for i in range(2)]
    from_y = [[inside[2 + i] * F32(s) for s in scaled] for i in range(2)]
    for x in range(12):
        for g in range(2):
            lows = [before_y[x, j * 2 + g] for j in range(6)]
            highs = [after_y[x, j * 2 + g] for j in range(6)]
            for yi in range(6):
                n = yi * 2 + g
                total = acc[x, n]
                for k in range(yi + 1, 7):
                    total = total + from_y[0][k] * lows[6 + yi - k]
                for k in range(6 - yi, 7):
                    total = total + from_y[1][k] * highs[yi + k - 6]
                if x < 6:
                    for k in range(x + 1, 7):
                        total = total + from_x[0][k] * before_x[6 + x - k, n]
                else:
                    for k in range(12 - x, 7):
                        total = total + from_x[1][k] * after_x[x + k - 12, n]
                full[x, n] = total
                if halves:
                    halves[x // 6][x % 6, n] = total


def bricks_body(place, low, high, next_low, last_high, out, rows, sem):
    first = place[0] == 0
    for xi in range(6):
        for yi in range(6):
            for g in range(2):
                n = yi * 2 + g
                start = g * 288 + xi * 6 + yi
                rows[pl.ds(start, 8, stride=36), :] = jnp.where(first, low[xi, n], last_high[xi, n])
                rows[pl.ds(576 + start, 8, stride=36), :] = jnp.where(first, next_low[xi, n], high[xi, n])
    write = pltpu.make_async_copy(rows, out, sem)
    write.start()
    write.wait()


def stack(parts, half, xi, yi):
    left = [p[half][xi, yi * 2 + g] for p in parts for g in range(2)]
    right = [p[half][xi, yi * 2 + 2 + g] for p in parts for g in range(2)]
    return jnp.concatenate([jnp.concatenate(left, axis=0), jnp.concatenate(right, axis=0)], axis=1)


def products(left, right):
    total = None
    for half in range(2):
        for xi in range(6):
            for yi in range(0, 6, 2):
                term = lax.dot_general(
                    stack(left, half, xi, yi),
                    stack(right, half, xi, yi),
                    (((1,), (1,)), ((), ())),
                    precision=lax.Precision.HIGHEST,
                    preferred_element_type=F32,
                )
                total = term if total is None else total + term
    return total


def halves_of(full):
    return full.at[pl.ds(0, 6)], full.at[pl.ds(6, 6)]


def near_gram_body(low, high, applied, next_low, next_high, last_low, last_high, out):
    mine = (low, high)
    total = products([mine, halves_of(applied)], [mine, (next_low, next_high), (last_low, last_high)])
    out[...] = jnp.concatenate([total, jnp.zeros((32, 80), F32)], axis=1)


def far_gram_body(place, low, high, applied, far_low, far_high, near, copies):
    far = products([(low, high), halves_of(applied)], [(far_low, far_high)])
    blocks = [near[:, 0:16], near[:, 16:32], far, near[:, 32:48]]
    total = None
    for p in range(4):
        turned = jnp.concatenate([blocks[(b - p) % 4] for b in range(4)], axis=1)
        total = turned if total is None else jnp.where(place[1] == p, turned, total)
    packed = jnp.concatenate([total[:16], total[16:]], axis=1)
    for n in range(16):
        copies[n] = packed


def sum_body(parts, copies):
    for half in range(2):
        total = parts[half * 8]
        for n in range(1, 8):
            total = total + parts[half * 8 + n]
        for n in range(8):
            copies[n, half * 16 : half * 16 + 16] = total


def finish_body(parts, energy, margin):
    total = parts[0]
    for n in range(1, 8):
        total = total + parts[n]
    total = total * F32(1.0 / CELLS)
    margin[...] = total[:, :64]
    energy[...] = total[:, 64:]


UP = [(i, (i + 1) % 8) for i in range(8)]
DOWN = [(i, (i + 7) % 8) for i in range(8)]
SWAP = [(0, 1), (1, 0)]
RING = ("xl", "xh")
SPOT = (0, 2, 1, 3)
NEXT = [(SPOT[i], SPOT[(i + 1) % 4]) for i in range(4)]
LAST = [(SPOT[i], SPOT[(i + 3) % 4]) for i in range(4)]
ROWS = ("y", "core")


def local(orbitals, potential):
    position_x = lax.axis_index("z")
    position_y = lax.axis_index(ROWS)
    side = lax.axis_index("xl")
    inside = jnp.stack([position_x > 0, position_x < 7, position_y > 0, position_y < 7]).astype(F32)
    place = jnp.stack([side, 2 * lax.axis_index("xh") + side]).astype(jnp.int32)

    half_width = (upper_edge - cut_edge) / 2.0
    centre = (upper_edge + cut_edge) / 2.0
    sigma_first = half_width / (lower_edge - centre)
    tau_value = 2.0 / sigma_first
    sigma_second = 1.0 / (tau_value - sigma_first)
    sigma_third = 1.0 / (tau_value - sigma_second)
    first = (sigma_first / half_width, centre, 0.0)
    second = (2.0 * sigma_second / half_width, centre, sigma_first * sigma_second)
    third = (2.0 * sigma_third / half_width, centre, sigma_second * sigma_third)
    plain = (1.0, 0.0, 0.0)

    mine = orbitals.reshape(1152, 128)
    own_field = potential.reshape(36, 128)
    received = lax.ppermute(lax.dynamic_slice_in_dim(mine, (1 - side) * 576, 576), "xl", SWAP)
    other_field = lax.ppermute(own_field, "xl", SWAP)
    keep = lax.dynamic_slice_in_dim(mine, side * 576, 576)
    full, low, high, field = call(
        assemble_body,
        [FULL, HALF, HALF, jax.ShapeDtypeStruct((12, 6, 8, 128), F32)],
        [place, keep, received, own_field, other_field],
        [SM] + [VM] * 4,
    )

    def step(numbers, planes, previous, outs):
        full, low, high = planes
        halos = (
            lax.ppermute(full, ROWS, UP),
            lax.ppermute(full, ROWS, DOWN),
            lax.ppermute(high, "z", UP),
            lax.ppermute(low, "z", DOWN),
        )

        def interior(*refs):
            interior_body(*numbers, *refs)

        acc = call(interior, FULL, [full, field, *previous], flops=400_000_000)

        def edge(*refs):
            edge_body(numbers[0], *refs)

        return call(edge, outs, [inside, acc, *halos[2:], *halos[:2]], [SM] + [VM] * 5)

    y0 = (full, low, high)
    y1 = step(first, y0, (), [FULL, HALF, HALF])
    y2 = step(second, y1, (y0[0],), [FULL, HALF, HALF])
    y3 = step(third, y2, (y1[0],), [FULL, HALF, HALF])
    applied = step(plain, y3, (), [FULL])[0]
    full, low, high = y3
    next_low = lax.ppermute(low, RING, LAST)
    last_high = lax.ppermute(high, RING, NEXT)
    next_high = lax.ppermute(high, RING, LAST)
    last_low = lax.ppermute(low, RING, NEXT)
    far_low = lax.ppermute(next_low, RING, LAST)
    far_high = lax.ppermute(last_high, RING, NEXT)
    filtered = call(
        bricks_body,
        jax.ShapeDtypeStruct((1152, 128), F32),
        [place, low, high, next_low, last_high],
        [SM] + [VM] * 4,
        out_specs=pl.BlockSpec(memory_space=pl.ANY),
        scratch=[pltpu.VMEM((1152, 128), F32), pltpu.SemaphoreType.DMA],
        flops=400_000_000,
    )
    near = call(
        near_gram_body,
        jax.ShapeDtypeStruct((32, 128), F32),
        [low, high, applied, next_low, next_high, last_low, last_high],
        flops=400_000_000,
    )
    copies = call(
        far_gram_body,
        jax.ShapeDtypeStruct((16, 16, 128), F32),
        [place, low, high, applied, far_low, far_high, near],
        [SM] + [VM] * 6,
    )
    parts = lax.all_to_all(copies, ("xl",) + ROWS, split_axis=0, concat_axis=0, tiled=True)
    copies = call(sum_body, jax.ShapeDtypeStruct((8, 32, 128), F32), [parts])
    parts = lax.all_to_all(copies, "z", split_axis=0, concat_axis=0, tiled=True)
    energy, margin = call(finish_body, [jax.ShapeDtypeStruct((32, 64), F32)] * 2, [parts])
    return filtered.reshape(32, 1, 6, 6, 128), energy, margin


def solution(mesh):
    fine = Mesh(mesh.devices.reshape(8, 2, 4, 2, 2), ("z", "xl", "y", "core", "xh"))
    brick = ("z", "xl", "y", "core")
    return jax.shard_map(
        local,
        mesh=fine,
        in_specs=(P("xh", brick, None, None, None), P(brick, None, None, None)),
        out_specs=(P("xh", brick, None, None, None), P("xh", None), P("xh", None)),
        check_vma=False,
    )
```

```python
import jax
import jax.numpy as jnp
from jax import lax
from jax.experimental import pallas as pl
from jax.experimental.pallas import tpu as pltpu
from jax.sharding import Mesh, PartitionSpec as P

weights = (
    -5369.0 / 1800.0,
    12.0 / 7.0,
    -15.0 / 56.0,
    10.0 / 189.0,
    -1.0 / 112.0,
    2.0 / 825.0,
    -1.0 / 4752.0,
)
lower_edge = 0.0
cut_edge = 3.0
upper_edge = 13.0
CELLS = 96 * 48 * 128

VM = pl.BlockSpec(memory_space=pltpu.VMEM)
SM = pl.BlockSpec(memory_space=pltpu.SMEM)
PARAMS = pltpu.CompilerParams(vmem_limit_bytes=32 * 1024 * 1024)
F32 = jnp.float32

HALF = jax.ShapeDtypeStruct((6, 12, 8, 128), F32)
FULL = jax.ShapeDtypeStruct((12, 12, 8, 128), F32)


def call(body, outs, inputs, specs=None, out_specs=None, scratch=(), flops=1_000_000):
    return pl.pallas_call(
        body,
        out_shape=outs,
        in_specs=specs or [VM] * len(inputs),
        out_specs=out_specs or jax.tree.map(lambda _: VM, outs),
        scratch_shapes=scratch,
        compiler_params=PARAMS,
        cost_estimate=pl.CostEstimate(flops=flops, bytes_accessed=2_000_000, transcendentals=0),
    )(*inputs)


def assemble_body(place, mine, received, own_field, other_field, full, low, high, field):
    first = place[0] == 0
    for xi in range(6):
        for yi in range(6):
            r = xi * 6 + yi
            for g in range(2):
                rows = pl.ds(g * 288 + r, 8, stride=36)
                a = jnp.where(first, mine[rows, :], mine[pl.ds(576 + g * 288 + r, 8, stride=36), :])
                b = received[rows, :]
                n = yi * 2 + g
                left = jnp.where(first, a, b)
                right = jnp.where(first, b, a)
                full[xi, n] = left
                low[xi, n] = left
                full[6 + xi, n] = right
                high[xi, n] = right
            a = jnp.broadcast_to(own_field[pl.ds(r, 1), :], (8, 128))
            b = jnp.broadcast_to(other_field[pl.ds(r, 1), :], (8, 128))
            field[xi, yi] = jnp.where(first, a, b)
            field[6 + xi, yi] = jnp.where(first, b, a)


def interior_body(alpha, shift, beta, full, field, *refs):
    acc = refs[-1]
    scaled = [-0.5 * alpha * w for w in weights]
    row = lax.broadcasted_iota(jnp.int32, (128, 128), 0)
    column = lax.broadcasted_iota(jnp.int32, (128, 128), 1)
    distance = jnp.abs(row - column)
    band = jnp.zeros((128, 128), F32)
    for k in range(1, 7):
        band = jnp.where(distance == k, F32(scaled[k]), band)
    band = jnp.where(distance == 0, F32(3.0 * scaled[0] - alpha * shift), band)
    for x in range(12):
        along = jnp.dot(
            full[x].reshape(96, 128), band, precision=lax.Precision.HIGHEST, preferred_element_type=F32
        ).reshape(12, 8, 128)
        for g in range(2):
            line = [full[x, yi * 2 + g] for yi in range(6)]
            for yi in range(6):
                n = yi * 2 + g
                total = along[n] + field[x, yi] * F32(alpha) * line[yi]
                for k in range(1, 7):
                    near = [line[yi + s] for s in (k, -k) if 0 <= yi + s < 6]
                    near += [full[x + s, n] for s in (k, -k) if 0 <= x + s < 12]
                    if near:
                        pair = near[0]
                        for v in near[1:]:
                            pair = pair + v
                        total = total + F32(scaled[k]) * pair
                if len(refs) == 2:
                    total = total - F32(beta) * refs[0][x, n]
                acc[x, n] = total


def edge_body(alpha, inside, acc, before_x, after_x, before_y, after_y, full, *halves):
    scaled = [-0.5 * alpha * w for w in weights]
    from_x = [[inside[i] * F32(s) for s in scaled] for i in range(2)]
    from_y = [[inside[2 + i] * F32(s) for s in scaled] for i in range(2)]
    for x in range(12):
        for g in range(2):
            lows = [before_y[x, j * 2 + g] for j in range(6)]
            highs = [after_y[x, j * 2 + g] for j in range(6)]
            for yi in range(6):
                n = yi * 2 + g
                total = acc[x, n]
                for k in range(yi + 1, 7):
                    total = total + from_y[0][k] * lows[6 + yi - k]
                for k in range(6 - yi, 7):
                    total = total + from_y[1][k] * highs[yi + k - 6]
                if x < 6:
                    for k in range(x + 1, 7):
                        total = total + from_x[0][k] * before_x[6 + x - k, n]
                else:
                    for k in range(12 - x, 7):
                        total = total + from_x[1][k] * after_x[x + k - 12, n]
                full[x, n] = total
                if halves:
                    halves[x // 6][x % 6, n] = total


def bricks_body(place, low, high, next_low, last_high, out, rows, sem):
    first = place[0] == 0
    for xi in range(6):
        for yi in range(6):
            for g in range(2):
                n = yi * 2 + g
                start = g * 288 + xi * 6 + yi
                rows[pl.ds(start, 8, stride=36), :] = jnp.where(first, low[xi, n], last_high[xi, n])
                rows[pl.ds(576 + start, 8, stride=36), :] = jnp.where(first, next_low[xi, n], high[xi, n])
    write = pltpu.make_async_copy(rows, out, sem)
    write.start()
    write.wait()


def stack(parts, half, xi, yi):
    left = [p[half][xi, yi * 2 + g] for p in parts for g in range(2)]
    right = [p[half][xi, yi * 2 + 2 + g] for p in parts for g in range(2)]
    return jnp.concatenate([jnp.concatenate(left, axis=0), jnp.concatenate(right, axis=0)], axis=1)


def products(left, right, halves=(0, 1)):
    total = None
    for half in halves:
        for xi in range(6):
            for yi in range(0, 6, 2):
                term = lax.dot_general(
                    stack(left, half, xi, yi),
                    stack(right, half, xi, yi),
                    (((1,), (1,)), ((), ())),
                    precision=lax.Precision.HIGHEST,
                    preferred_element_type=F32,
                )
                total = term if total is None else total + term
    return total


def halves_of(full):
    return full.at[pl.ds(0, 6)], full.at[pl.ds(6, 6)]


def near_gram_body(low, high, applied, next_low, next_high, last_low, last_high, out):
    mine = (low, high)
    total = products([mine, halves_of(applied)], [mine, (next_low, next_high), (last_low, last_high)])
    out[...] = jnp.concatenate([total, jnp.zeros((32, 80), F32)], axis=1)


def far_low_body(low, high, applied, far_low, out):
    far = products([(low, high), halves_of(applied)], [(far_low, None)], (0,))
    out[...] = jnp.concatenate([far, jnp.zeros((32, 112), F32)], axis=1)


def far_gram_body(place, low, high, applied, far_high, near, far_part, copies):
    far = far_part[:, 0:16] + products([(low, high), halves_of(applied)], [(None, far_high)], (1,))
    blocks = [near[:, 0:16], near[:, 16:32], far, near[:, 32:48]]
    total = None
    for p in range(4):
        turned = jnp.concatenate([blocks[(b - p) % 4] for b in range(4)], axis=1)
        total = turned if total is None else jnp.where(place[1] == p, turned, total)
    packed = jnp.concatenate([total[:16], total[16:]], axis=1)
    for n in range(16):
        copies[n] = packed


def sum_body(parts, copies):
    for half in range(2):
        total = parts[half * 8]
        for n in range(1, 8):
            total = total + parts[half * 8 + n]
        for n in range(8):
            copies[n, half * 16 : half * 16 + 16] = total


def finish_body(parts, energy, margin):
    total = parts[0]
    for n in range(1, 8):
        total = total + parts[n]
    total = total * F32(1.0 / CELLS)
    margin[...] = total[:, :64]
    energy[...] = total[:, 64:]


UP = [(i, (i + 1) % 8) for i in range(8)]
DOWN = [(i, (i + 7) % 8) for i in range(8)]
SWAP = [(0, 1), (1, 0)]
RING = ("xl", "xh")
SPOT = (0, 2, 1, 3)
NEXT = [(SPOT[i], SPOT[(i + 1) % 4]) for i in range(4)]
LAST = [(SPOT[i], SPOT[(i + 3) % 4]) for i in range(4)]
ROWS = ("y", "core")


def local(orbitals, potential):
    position_x = lax.axis_index("z")
    position_y = lax.axis_index(ROWS)
    side = lax.axis_index("xl")
    inside = jnp.stack([position_x > 0, position_x < 7, position_y > 0, position_y < 7]).astype(F32)
    place = jnp.stack([side, 2 * lax.axis_index("xh") + side]).astype(jnp.int32)

    half_width = (upper_edge - cut_edge) / 2.0
    centre = (upper_edge + cut_edge) / 2.0
    sigma_first = half_width / (lower_edge - centre)
    tau_value = 2.0 / sigma_first
    sigma_second = 1.0 / (tau_value - sigma_first)
    sigma_third = 1.0 / (tau_value - sigma_second)
    first = (sigma_first / half_width, centre, 0.0)
    second = (2.0 * sigma_second / half_width, centre, sigma_first * sigma_second)
    third = (2.0 * sigma_third / half_width, centre, sigma_second * sigma_third)
    plain = (1.0, 0.0, 0.0)

    mine = orbitals.reshape(1152, 128)
    own_field = potential.reshape(36, 128)
    received = lax.ppermute(lax.dynamic_slice_in_dim(mine, (1 - side) * 576, 576), "xl", SWAP)
    other_field = lax.ppermute(own_field, "xl", SWAP)
    full, low, high, field = call(
        assemble_body,
        [FULL, HALF, HALF, jax.ShapeDtypeStruct((12, 6, 8, 128), F32)],
        [place, mine, received, own_field, other_field],
        [SM] + [VM] * 4,
    )

    def step(numbers, planes, previous, outs, others=()):
        full, low, high = planes
        halos = (
            lax.ppermute(full, ROWS, UP),
            lax.ppermute(full, ROWS, DOWN),
            lax.ppermute(high, "z", UP),
            lax.ppermute(low, "z", DOWN),
        )

        def interior(*refs):
            interior_body(*numbers, *refs)

        acc = call(interior, FULL, [full, field, *previous], flops=400_000_000)

        if others:
            acc = lax.optimization_barrier((acc, *others))[0]

        def edge(*refs):
            edge_body(numbers[0], *refs)

        return call(edge, outs, [inside, acc, *halos[2:], *halos[:2]], [SM] + [VM] * 5)

    y0 = (full, low, high)
    y1 = step(first, y0, (), [FULL, HALF, HALF])
    y2 = step(second, y1, (y0[0],), [FULL, HALF, HALF])
    y3 = step(third, y2, (y1[0],), [FULL, HALF, HALF])
    full, low, high = y3
    next_low = lax.ppermute(low, RING, LAST)
    last_high = lax.ppermute(high, RING, NEXT)
    next_high = lax.ppermute(high, RING, LAST)
    last_low = lax.ppermute(low, RING, NEXT)
    applied = step(plain, y3, (), [FULL], (next_low, last_high, next_high, last_low))[0]
    far_low = lax.ppermute(next_low, RING, LAST)
    far_high = lax.ppermute(last_high, RING, NEXT)
    filtered = call(
        bricks_body,
        jax.ShapeDtypeStruct((1152, 128), F32),
        [place, low, high, next_low, last_high],
        [SM] + [VM] * 4,
        out_specs=pl.BlockSpec(memory_space=pl.ANY),
        scratch=[pltpu.VMEM((1152, 128), F32), pltpu.SemaphoreType.DMA],
        flops=400_000_000,
    )
    near = call(
        near_gram_body,
        jax.ShapeDtypeStruct((32, 128), F32),
        [low, high, applied, next_low, next_high, last_low, last_high],
        flops=400_000_000,
    )
    far_part = call(
        far_low_body,
        jax.ShapeDtypeStruct((32, 128), F32),
        [low, high, applied, far_low],
        flops=400_000_000,
    )
    copies = call(
        far_gram_body,
        jax.ShapeDtypeStruct((16, 16, 128), F32),
        [place, low, high, applied, far_high, near, far_part],
        [SM] + [VM] * 6,
    )
    parts = lax.all_to_all(copies, ("xl",) + ROWS, split_axis=0, concat_axis=0, tiled=True)
    copies = call(sum_body, jax.ShapeDtypeStruct((8, 32, 128), F32), [parts])
    parts = lax.all_to_all(copies, "z", split_axis=0, concat_axis=0, tiled=True)
    energy, margin = call(finish_body, [jax.ShapeDtypeStruct((32, 64), F32)] * 2, [parts])
    return filtered.reshape(32, 1, 6, 6, 128), energy, margin


def solution(mesh):
    fine = Mesh(mesh.devices.reshape(8, 2, 4, 2, 2), ("z", "xl", "y", "core", "xh"))
    brick = ("z", "xl", "y", "core")
    return jax.shard_map(
        local,
        mesh=fine,
        in_specs=(P("xh", brick, None, None, None), P(brick, None, None, None)),
        out_specs=(P("xh", brick, None, None, None), P("xh", None), P("xh", None)),
        check_vma=False,
    )
```

```python
import jax
import jax.numpy as jnp
from jax import lax
from jax.experimental import pallas as pl
from jax.experimental.pallas import tpu as pltpu
from jax.sharding import Mesh, PartitionSpec as P

weights = (
    -5369.0 / 1800.0,
    12.0 / 7.0,
    -15.0 / 56.0,
    10.0 / 189.0,
    -1.0 / 112.0,
    2.0 / 825.0,
    -1.0 / 4752.0,
)
lower_edge = 0.0
cut_edge = 3.0
upper_edge = 13.0
CELLS = 96 * 48 * 128

VM = pl.BlockSpec(memory_space=pltpu.VMEM)
SM = pl.BlockSpec(memory_space=pltpu.SMEM)
PARAMS = pltpu.CompilerParams(vmem_limit_bytes=32 * 1024 * 1024)
F32 = jnp.float32

HALF = jax.ShapeDtypeStruct((6, 12, 8, 128), F32)
FULL = jax.ShapeDtypeStruct((12, 12, 8, 128), F32)


def call(body, outs, inputs, specs=None, out_specs=None, scratch=(), flops=1_000_000):
    return pl.pallas_call(
        body,
        out_shape=outs,
        in_specs=specs or [VM] * len(inputs),
        out_specs=out_specs or jax.tree.map(lambda _: VM, outs),
        scratch_shapes=scratch,
        compiler_params=PARAMS,
        cost_estimate=pl.CostEstimate(flops=flops, bytes_accessed=2_000_000, transcendentals=0),
    )(*inputs)


def assemble_body(place, mine, received, own_field, other_field, full, low, high, field):
    first = place[0] == 0
    for xi in range(6):
        for yi in range(6):
            r = xi * 6 + yi
            for g in range(2):
                rows = pl.ds(g * 288 + r, 8, stride=36)
                a = jnp.where(first, mine[rows, :], mine[pl.ds(576 + g * 288 + r, 8, stride=36), :])
                b = received[rows, :]
                n = yi * 2 + g
                left = jnp.where(first, a, b)
                right = jnp.where(first, b, a)
                full[xi, n] = left
                low[xi, n] = left
                full[6 + xi, n] = right
                high[xi, n] = right
            a = jnp.broadcast_to(own_field[pl.ds(r, 1), :], (8, 128))
            b = jnp.broadcast_to(other_field[pl.ds(r, 1), :], (8, 128))
            field[xi, yi] = jnp.where(first, a, b)
            field[6 + xi, yi] = jnp.where(first, b, a)


def interior_body(alpha, shift, beta, full, field, *refs):
    acc = refs[-1]
    scaled = [-0.5 * alpha * w for w in weights]
    row = lax.broadcasted_iota(jnp.int32, (128, 128), 0)
    column = lax.broadcasted_iota(jnp.int32, (128, 128), 1)
    distance = jnp.abs(row - column)
    band = jnp.zeros((128, 128), F32)
    for k in range(1, 7):
        band = jnp.where(distance == k, F32(scaled[k]), band)
    band = jnp.where(distance == 0, F32(3.0 * scaled[0] - alpha * shift), band)
    for x in range(12):
        along = jnp.dot(
            full[x].reshape(96, 128), band, precision=lax.Precision.HIGHEST, preferred_element_type=F32
        ).reshape(12, 8, 128)
        for g in range(2):
            line = [full[x, yi * 2 + g] for yi in range(6)]
            for yi in range(6):
                n = yi * 2 + g
                total = along[n] + field[x, yi] * F32(alpha) * line[yi]
                for k in range(1, 7):
                    near = [line[yi + s] for s in (k, -k) if 0 <= yi + s < 6]
                    near += [full[x + s, n] for s in (k, -k) if 0 <= x + s < 12]
                    if near:
                        pair = near[0]
                        for v in near[1:]:
                            pair = pair + v
                        total = total + F32(scaled[k]) * pair
                if len(refs) == 2:
                    total = total - F32(beta) * refs[0][x, n]
                acc[x, n] = total


def edge_y_body(alpha, inside, acc, before, after, out):
    scaled = [-0.5 * alpha * w for w in weights]
    lower = [inside[2] * F32(s) for s in scaled]
    upper = [inside[3] * F32(s) for s in scaled]
    for x in range(12):
        for g in range(2):
            lows = [before[x, j * 2 + g] for j in range(6)]
            highs = [after[x, j * 2 + g] for j in range(6)]
            for yi in range(6):
                n = yi * 2 + g
                total = acc[x, n]
                for k in range(yi + 1, 7):
                    total = total + lower[k] * lows[6 + yi - k]
                for k in range(6 - yi, 7):
                    total = total + upper[k] * highs[yi + k - 6]
                out[x, n] = total


def edge_x_body(alpha, inside, acc, before, after, full, *halves):
    scaled = [-0.5 * alpha * w for w in weights]
    lower = [inside[0] * F32(s) for s in scaled]
    upper = [inside[1] * F32(s) for s in scaled]
    for n in range(12):
        lows = [before[j, n] for j in range(6)]
        highs = [after[j, n] for j in range(6)]
        for x in range(12):
            total = acc[x, n]
            if x < 6:
                for k in range(x + 1, 7):
                    total = total + lower[k] * lows[6 + x - k]
            else:
                for k in range(12 - x, 7):
                    total = total + upper[k] * highs[x + k - 12]
            full[x, n] = total
            if halves:
                halves[x // 6][x % 6, n] = total


def bricks_body(place, low, high, following, preceding, out, rows, sem):
    first = place[0] == 0
    for xi in range(6):
        for yi in range(6):
            for g in range(2):
                n = yi * 2 + g
                start = g * 288 + xi * 6 + yi
                rows[pl.ds(start, 8, stride=36), :] = jnp.where(first, low[xi, n], preceding[6 + xi, n])
                rows[pl.ds(576 + start, 8, stride=36), :] = jnp.where(first, following[xi, n], high[xi, n])
    write = pltpu.make_async_copy(rows, out, sem)
    write.start()
    write.wait()


def stack(parts, half, xi, yi):
    left = [p[half][xi, yi * 2 + g] for p in parts for g in range(2)]
    right = [p[half][xi, yi * 2 + 2 + g] for p in parts for g in range(2)]
    return jnp.concatenate([jnp.concatenate(left, axis=0), jnp.concatenate(right, axis=0)], axis=1)


def products(left, right, halves=(0, 1)):
    total = None
    for half in halves:
        for xi in range(6):
            for yi in range(0, 6, 2):
                term = lax.dot_general(
                    stack(left, half, xi, yi),
                    stack(right, half, xi, yi),
                    (((1,), (1,)), ((), ())),
                    precision=lax.Precision.HIGHEST,
                    preferred_element_type=F32,
                )
                total = term if total is None else total + term
    return total


def halves_of(full):
    return full.at[pl.ds(0, 6)], full.at[pl.ds(6, 6)]


def near_gram_body(low, high, applied, following, preceding, out):
    mine = (low, high)
    total = products([mine, halves_of(applied)], [mine, halves_of(following), halves_of(preceding)])
    out[...] = jnp.concatenate([total, jnp.zeros((32, 80), F32)], axis=1)


def far_low_body(low, high, applied, far_low, out):
    far = products([(low, high), halves_of(applied)], [(far_low, None)], (0,))
    out[...] = jnp.concatenate([far, jnp.zeros((32, 112), F32)], axis=1)


def far_gram_body(place, low, high, applied, far_high, near, far_part, copies):
    far = far_part[:, 0:16] + products([(low, high), halves_of(applied)], [(None, far_high)], (1,))
    blocks = [near[:, 0:16], near[:, 16:32], far, near[:, 32:48]]
    total = None
    for p in range(4):
        turned = jnp.concatenate([blocks[(b - p) % 4] for b in range(4)], axis=1)
        total = turned if total is None else jnp.where(place[1] == p, turned, total)
    packed = jnp.concatenate([total[:16], total[16:]], axis=1)
    for n in range(16):
        copies[n] = packed


def sum_body(parts, copies):
    for half in range(2):
        total = parts[half * 8]
        for n in range(1, 8):
            total = total + parts[half * 8 + n]
        for n in range(8):
            copies[n, half * 16 : half * 16 + 16] = total


def finish_body(parts, energy, margin):
    total = parts[0]
    for n in range(1, 8):
        total = total + parts[n]
    total = total * F32(1.0 / CELLS)
    margin[...] = total[:, :64]
    energy[...] = total[:, 64:]


UP = [(i, (i + 1) % 8) for i in range(8)]
DOWN = [(i, (i + 7) % 8) for i in range(8)]
SWAP = [(0, 1), (1, 0)]
RING = ("xl", "xh")
SPOT = (0, 2, 1, 3)
NEXT = [(SPOT[i], SPOT[(i + 1) % 4]) for i in range(4)]
LAST = [(SPOT[i], SPOT[(i + 3) % 4]) for i in range(4)]
ROWS = ("y", "core")


def local(orbitals, potential):
    position_x = lax.axis_index("z")
    position_y = lax.axis_index(ROWS)
    side = lax.axis_index("xl")
    inside = jnp.stack([position_x > 0, position_x < 7, position_y > 0, position_y < 7]).astype(F32)
    place = jnp.stack([side, 2 * lax.axis_index("xh") + side]).astype(jnp.int32)

    half_width = (upper_edge - cut_edge) / 2.0
    centre = (upper_edge + cut_edge) / 2.0
    sigma_first = half_width / (lower_edge - centre)
    tau_value = 2.0 / sigma_first
    sigma_second = 1.0 / (tau_value - sigma_first)
    sigma_third = 1.0 / (tau_value - sigma_second)
    first = (sigma_first / half_width, centre, 0.0)
    second = (2.0 * sigma_second / half_width, centre, sigma_first * sigma_second)
    third = (2.0 * sigma_third / half_width, centre, sigma_second * sigma_third)
    plain = (1.0, 0.0, 0.0)

    mine = orbitals.reshape(1152, 128)
    own_field = potential.reshape(36, 128)
    received = lax.ppermute(lax.dynamic_slice_in_dim(mine, (1 - side) * 576, 576), "xl", SWAP)
    other_field = lax.ppermute(own_field, "xl", SWAP)
    full, low, high, field = call(
        assemble_body,
        [FULL, HALF, HALF, jax.ShapeDtypeStruct((12, 6, 8, 128), F32)],
        [place, mine, received, own_field, other_field],
        [SM] + [VM] * 4,
    )

    def step(numbers, planes, previous, outs, last=False):
        full, low, high = planes
        before_x = lax.ppermute(high, "z", UP)
        after_x = lax.ppermute(low, "z", DOWN)
        later = full
        if last:
            later = lax.optimization_barrier((full, before_x))[0]
        halos = (lax.ppermute(full, ROWS, UP), lax.ppermute(later, ROWS, DOWN), before_x, after_x)

        def interior(*refs):
            interior_body(*numbers, *refs)

        acc = call(interior, FULL, [full, field, *previous], flops=400_000_000)

        def edge_y(*refs):
            edge_y_body(numbers[0], *refs)

        def edge_x(*refs):
            edge_x_body(numbers[0], *refs)

        acc = call(edge_y, FULL, [inside, acc, *halos[:2]], [SM] + [VM] * 3, flops=200_000_000)
        return call(edge_x, outs, [inside, acc, *halos[2:]], [SM] + [VM] * 3)

    y0 = (full, low, high)
    y1 = step(first, y0, (), [FULL, HALF, HALF])
    y2 = step(second, y1, (y0[0],), [FULL, HALF, HALF])
    y3 = step(third, y2, (y1[0],), [FULL, HALF, HALF])
    full, low, high = y3
    following = lax.ppermute(full, RING, LAST)
    preceding = lax.ppermute(full, RING, NEXT)
    far_low = lax.ppermute(following[:6], RING, LAST)
    far_high = lax.ppermute(preceding[6:], RING, NEXT)
    applied = step(plain, y3, (), [FULL], True)[0]
    filtered = call(
        bricks_body,
        jax.ShapeDtypeStruct((1152, 128), F32),
        [place, low, high, following, preceding],
        [SM] + [VM] * 4,
        out_specs=pl.BlockSpec(memory_space=pl.ANY),
        scratch=[pltpu.VMEM((1152, 128), F32), pltpu.SemaphoreType.DMA],
        flops=400_000_000,
    )
    near = call(
        near_gram_body,
        jax.ShapeDtypeStruct((32, 128), F32),
        [low, high, applied, following, preceding],
        flops=400_000_000,
    )
    far_part = call(
        far_low_body,
        jax.ShapeDtypeStruct((32, 128), F32),
        [low, high, applied, far_low],
        flops=400_000_000,
    )
    copies = call(
        far_gram_body,
        jax.ShapeDtypeStruct((16, 16, 128), F32),
        [place, low, high, applied, far_high, near, far_part],
        [SM] + [VM] * 6,
    )
    parts = lax.all_to_all(copies, ("xl",) + ROWS, split_axis=0, concat_axis=0, tiled=True)
    copies = call(sum_body, jax.ShapeDtypeStruct((8, 32, 128), F32), [parts])
    parts = lax.all_to_all(copies, "z", split_axis=0, concat_axis=0, tiled=True)
    energy, margin = call(finish_body, [jax.ShapeDtypeStruct((32, 64), F32)] * 2, [parts])
    return filtered.reshape(32, 1, 6, 6, 128), energy, margin


def solution(mesh):
    fine = Mesh(mesh.devices.reshape(8, 2, 4, 2, 2), ("z", "xl", "y", "core", "xh"))
    brick = ("z", "xl", "y", "core")
    return jax.shard_map(
        local,
        mesh=fine,
        in_specs=(P("xh", brick, None, None, None), P(brick, None, None, None)),
        out_specs=(P("xh", brick, None, None, None), P("xh", None), P("xh", None)),
        check_vma=False,
    )
```

```python
import jax
import jax.numpy as jnp
from jax import lax
from jax.experimental import pallas as pl
from jax.experimental.pallas import tpu as pltpu
from jax.sharding import Mesh, PartitionSpec as P

weights = (
    -5369.0 / 1800.0,
    12.0 / 7.0,
    -15.0 / 56.0,
    10.0 / 189.0,
    -1.0 / 112.0,
    2.0 / 825.0,
    -1.0 / 4752.0,
)
lower_edge = 0.0
cut_edge = 3.0
upper_edge = 13.0
CELLS = 96 * 48 * 128

VM = pl.BlockSpec(memory_space=pltpu.VMEM)
SM = pl.BlockSpec(memory_space=pltpu.SMEM)
PARAMS = pltpu.CompilerParams(vmem_limit_bytes=8 * 1024 * 1024)
F32 = jnp.float32

HALF = jax.ShapeDtypeStruct((6, 12, 8, 128), F32)
FULL = jax.ShapeDtypeStruct((12, 12, 8, 128), F32)


def call(body, outs, inputs, specs=None, out_specs=None, scratch=(), flops=1_000_000):
    return pl.pallas_call(
        body,
        out_shape=outs,
        in_specs=specs or [VM] * len(inputs),
        out_specs=out_specs or jax.tree.map(lambda _: VM, outs),
        scratch_shapes=scratch,
        compiler_params=PARAMS,
        cost_estimate=pl.CostEstimate(flops=flops, bytes_accessed=2_000_000, transcendentals=0),
    )(*inputs)


def assemble_body(place, mine, received, own_field, other_field, full, low, high, field):
    first = place[0] == 0
    for xi in range(6):
        for yi in range(6):
            r = xi * 6 + yi
            for g in range(2):
                rows = pl.ds(g * 288 + r, 8, stride=36)
                a = jnp.where(first, mine[rows, :], mine[pl.ds(576 + g * 288 + r, 8, stride=36), :])
                b = received[rows, :]
                n = yi * 2 + g
                left = jnp.where(first, a, b)
                right = jnp.where(first, b, a)
                full[xi, n] = left
                low[xi, n] = left
                full[6 + xi, n] = right
                high[xi, n] = right
            a = jnp.broadcast_to(own_field[pl.ds(r, 1), :], (8, 128))
            b = jnp.broadcast_to(other_field[pl.ds(r, 1), :], (8, 128))
            field[xi, yi] = jnp.where(first, a, b)
            field[6 + xi, yi] = jnp.where(first, b, a)


def interior_body(alpha, shift, beta, full, field, *refs):
    acc = refs[-1]
    scaled = [-0.5 * alpha * w for w in weights]
    row = lax.broadcasted_iota(jnp.int32, (128, 128), 0)
    column = lax.broadcasted_iota(jnp.int32, (128, 128), 1)
    distance = jnp.abs(row - column)
    band = jnp.zeros((128, 128), F32)
    for k in range(1, 7):
        band = jnp.where(distance == k, F32(scaled[k]), band)
    band = jnp.where(distance == 0, F32(3.0 * scaled[0] - alpha * shift), band)
    for x in range(12):
        along = jnp.dot(
            full[x].reshape(96, 128), band, precision=lax.Precision.HIGHEST, preferred_element_type=F32
        ).reshape(12, 8, 128)
        for g in range(2):
            line = [full[x, yi * 2 + g] for yi in range(6)]
            for yi in range(6):
                n = yi * 2 + g
                total = along[n] + field[x, yi] * F32(alpha) * line[yi]
                for k in range(1, 7):
                    near = [line[yi + s] for s in (k, -k) if 0 <= yi + s < 6]
                    near += [full[x + s, n] for s in (k, -k) if 0 <= x + s < 12]
                    if near:
                        pair = near[0]
                        for v in near[1:]:
                            pair = pair + v
                        total = total + F32(scaled[k]) * pair
                if len(refs) == 2:
                    total = total - F32(beta) * refs[0][x, n]
                acc[x, n] = total


def edge_y_body(alpha, inside, acc, before, after, out):
    scaled = [-0.5 * alpha * w for w in weights]
    lower = [inside[2] * F32(s) for s in scaled]
    upper = [inside[3] * F32(s) for s in scaled]
    for x in range(12):
        for g in range(2):
            lows = [before[x, j * 2 + g] for j in range(6)]
            highs = [after[x, j * 2 + g] for j in range(6)]
            for yi in range(6):
                n = yi * 2 + g
                total = acc[x, n]
                for k in range(yi + 1, 7):
                    total = total + lower[k] * lows[6 + yi - k]
                for k in range(6 - yi, 7):
                    total = total + upper[k] * highs[yi + k - 6]
                out[x, n] = total


def edge_x_body(alpha, inside, acc, before, after, full, *halves):
    scaled = [-0.5 * alpha * w for w in weights]
    lower = [inside[0] * F32(s) for s in scaled]
    upper = [inside[1] * F32(s) for s in scaled]
    for n in range(12):
        lows = [before[j, n] for j in range(6)]
        highs = [after[j, n] for j in range(6)]
        for x in range(12):
            total = acc[x, n]
            if x < 6:
                for k in range(x + 1, 7):
                    total = total + lower[k] * lows[6 + x - k]
            else:
                for k in range(12 - x, 7):
                    total = total + upper[k] * highs[x + k - 12]
            full[x, n] = total
            if halves:
                halves[x // 6][x % 6, n] = total


def bricks_body(place, low, high, following, preceding, out, rows, sem):
    first = place[0] == 0
    for xi in range(6):
        for yi in range(6):
            for g in range(2):
                n = yi * 2 + g
                start = g * 288 + xi * 6 + yi
                rows[pl.ds(start, 8, stride=36), :] = jnp.where(first, low[xi, n], preceding[6 + xi, n])
                rows[pl.ds(576 + start, 8, stride=36), :] = jnp.where(first, following[xi, n], high[xi, n])
    write = pltpu.make_async_copy(rows, out, sem)
    write.start()
    write.wait()


def stack(parts, half, xi, yi):
    left = [p[half][xi, yi * 2 + g] for p in parts for g in range(2)]
    right = [p[half][xi, yi * 2 + 2 + g] for p in parts for g in range(2)]
    return jnp.concatenate([jnp.concatenate(left, axis=0), jnp.concatenate(right, axis=0)], axis=1)


def products(left, right, halves=(0, 1)):
    total = None
    for half in halves:
        for xi in range(6):
            for yi in range(0, 6, 2):
                term = lax.dot_general(
                    stack(left, half, xi, yi),
                    stack(right, half, xi, yi),
                    (((1,), (1,)), ((), ())),
                    precision=lax.Precision.HIGHEST,
                    preferred_element_type=F32,
                )
                total = term if total is None else total + term
    return total


def halves_of(full):
    return full.at[pl.ds(0, 6)], full.at[pl.ds(6, 6)]


def near_gram_body(low, high, applied, following, preceding, out):
    mine = (low, high)
    total = products([mine, halves_of(applied)], [mine, halves_of(following), halves_of(preceding)])
    out[...] = jnp.concatenate([total, jnp.zeros((32, 80), F32)], axis=1)


def far_low_body(low, high, applied, far_low, out):
    far = products([(low, high), halves_of(applied)], [(far_low, None)], (0,))
    out[...] = jnp.concatenate([far, jnp.zeros((32, 112), F32)], axis=1)


def far_gram_body(place, low, high, applied, far_high, near, far_part, copies):
    far = far_part[:, 0:16] + products([(low, high), halves_of(applied)], [(None, far_high)], (1,))
    blocks = [near[:, 0:16], near[:, 16:32], far, near[:, 32:48]]
    total = None
    for p in range(4):
        turned = jnp.concatenate([blocks[(b - p) % 4] for b in range(4)], axis=1)
        total = turned if total is None else jnp.where(place[1] == p, turned, total)
    packed = jnp.concatenate([total[:16], total[16:]], axis=1)
    for n in range(16):
        copies[n] = packed


def sum_body(parts, copies):
    for half in range(2):
        total = parts[half * 8]
        for n in range(1, 8):
            total = total + parts[half * 8 + n]
        for n in range(8):
            copies[n, half * 16 : half * 16 + 16] = total


def finish_body(parts, energy, margin):
    total = parts[0]
    for n in range(1, 8):
        total = total + parts[n]
    total = total * F32(1.0 / CELLS)
    margin[...] = total[:, :64]
    energy[...] = total[:, 64:]


UP = [(i, (i + 1) % 8) for i in range(8)]
DOWN = [(i, (i + 7) % 8) for i in range(8)]
SWAP = [(0, 1), (1, 0)]
RING = ("xl", "xh")
SPOT = (0, 2, 1, 3)
NEXT = [(SPOT[i], SPOT[(i + 1) % 4]) for i in range(4)]
LAST = [(SPOT[i], SPOT[(i + 3) % 4]) for i in range(4)]
ROWS = ("y", "core")


def local(orbitals, potential):
    position_x = lax.axis_index("z")
    position_y = lax.axis_index(ROWS)
    side = lax.axis_index("xl")
    inside = jnp.stack([position_x > 0, position_x < 7, position_y > 0, position_y < 7]).astype(F32)
    place = jnp.stack([side, 2 * lax.axis_index("xh") + side]).astype(jnp.int32)

    half_width = (upper_edge - cut_edge) / 2.0
    centre = (upper_edge + cut_edge) / 2.0
    sigma_first = half_width / (lower_edge - centre)
    tau_value = 2.0 / sigma_first
    sigma_second = 1.0 / (tau_value - sigma_first)
    sigma_third = 1.0 / (tau_value - sigma_second)
    first = (sigma_first / half_width, centre, 0.0)
    second = (2.0 * sigma_second / half_width, centre, sigma_first * sigma_second)
    third = (2.0 * sigma_third / half_width, centre, sigma_second * sigma_third)
    plain = (1.0, 0.0, 0.0)

    mine = orbitals.reshape(1152, 128)
    own_field = potential.reshape(36, 128)
    received = lax.ppermute(lax.dynamic_slice_in_dim(mine, (1 - side) * 576, 576), "xl", SWAP)
    other_field = lax.ppermute(own_field, "xl", SWAP)
    full, low, high, field = call(
        assemble_body,
        [FULL, HALF, HALF, jax.ShapeDtypeStruct((12, 6, 8, 128), F32)],
        [place, mine, received, own_field, other_field],
        [SM] + [VM] * 4,
    )

    def step(numbers, planes, previous, outs, last=False):
        full, low, high = planes
        before_x = lax.ppermute(high, "z", UP)
        after_x = lax.ppermute(low, "z", DOWN)
        later = full
        if last:
            later = lax.optimization_barrier((full, before_x))[0]
        halos = (lax.ppermute(full, ROWS, UP), lax.ppermute(later, ROWS, DOWN), before_x, after_x)

        def interior(*refs):
            interior_body(*numbers, *refs)

        acc = call(interior, FULL, [full, field, *previous], flops=400_000_000)

        def edge_y(*refs):
            edge_y_body(numbers[0], *refs)

        def edge_x(*refs):
            edge_x_body(numbers[0], *refs)

        acc = call(edge_y, FULL, [inside, acc, *halos[:2]], [SM] + [VM] * 3, flops=200_000_000)
        return call(edge_x, outs, [inside, acc, *halos[2:]], [SM] + [VM] * 3)

    y0 = (full, low, high)
    y1 = step(first, y0, (), [FULL, HALF, HALF])
    y2 = step(second, y1, (y0[0],), [FULL, HALF, HALF])
    y3 = step(third, y2, (y1[0],), [FULL, HALF, HALF])
    full, low, high = y3
    following = lax.ppermute(full, RING, LAST)
    preceding = lax.ppermute(full, RING, NEXT)
    far_low = lax.ppermute(following[:6], RING, LAST)
    far_high = lax.ppermute(preceding[6:], RING, NEXT)
    applied = step(plain, y3, (), [FULL], True)[0]
    filtered = call(
        bricks_body,
        jax.ShapeDtypeStruct((1152, 128), F32),
        [place, low, high, following, preceding],
        [SM] + [VM] * 4,
        out_specs=pl.BlockSpec(memory_space=pl.ANY),
        scratch=[pltpu.VMEM((1152, 128), F32), pltpu.SemaphoreType.DMA],
        flops=400_000_000,
    )
    applied = lax.optimization_barrier((applied, filtered))[0]
    near = call(
        near_gram_body,
        jax.ShapeDtypeStruct((32, 128), F32),
        [low, high, applied, following, preceding],
        flops=400_000_000,
    )
    far_part = call(
        far_low_body,
        jax.ShapeDtypeStruct((32, 128), F32),
        [low, high, applied, far_low],
        flops=400_000_000,
    )
    copies = call(
        far_gram_body,
        jax.ShapeDtypeStruct((16, 16, 128), F32),
        [place, low, high, applied, far_high, near, far_part],
        [SM] + [VM] * 6,
    )
    parts = lax.all_to_all(copies, ("xl",) + ROWS, split_axis=0, concat_axis=0, tiled=True)
    copies = call(sum_body, jax.ShapeDtypeStruct((8, 32, 128), F32), [parts])
    parts = lax.all_to_all(copies, "z", split_axis=0, concat_axis=0, tiled=True)
    energy, margin = call(finish_body, [jax.ShapeDtypeStruct((32, 64), F32)] * 2, [parts])
    return filtered.reshape(32, 1, 6, 6, 128), energy, margin


def solution(mesh):
    fine = Mesh(mesh.devices.reshape(8, 2, 4, 2, 2), ("z", "xl", "y", "core", "xh"))
    brick = ("z", "xl", "y", "core")
    return jax.shard_map(
        local,
        mesh=fine,
        in_specs=(P("xh", brick, None, None, None), P(brick, None, None, None)),
        out_specs=(P("xh", brick, None, None, None), P("xh", None), P("xh", None)),
        check_vma=False,
    )
```

```python
import jax
import jax.numpy as jnp
from jax import lax
from jax.experimental import pallas as pl
from jax.experimental.pallas import tpu as pltpu
from jax.sharding import Mesh, PartitionSpec as P

weights = (
    -5369.0 / 1800.0,
    12.0 / 7.0,
    -15.0 / 56.0,
    10.0 / 189.0,
    -1.0 / 112.0,
    2.0 / 825.0,
    -1.0 / 4752.0,
)
lower_edge = 0.0
cut_edge = 3.0
upper_edge = 13.0
CELLS = 96 * 48 * 128

VM = pl.BlockSpec(memory_space=pltpu.VMEM)
SM = pl.BlockSpec(memory_space=pltpu.SMEM)
PARAMS = pltpu.CompilerParams(vmem_limit_bytes=8 * 1024 * 1024)
F32 = jnp.float32

HALF = jax.ShapeDtypeStruct((6, 12, 8, 128), F32)
FULL = jax.ShapeDtypeStruct((12, 12, 8, 128), F32)


def call(body, outs, inputs, specs=None, out_specs=None, scratch=(), flops=1_000_000):
    return pl.pallas_call(
        body,
        out_shape=outs,
        in_specs=specs or [VM] * len(inputs),
        out_specs=out_specs or jax.tree.map(lambda _: VM, outs),
        scratch_shapes=scratch,
        compiler_params=PARAMS,
        cost_estimate=pl.CostEstimate(flops=flops, bytes_accessed=2_000_000, transcendentals=0),
    )(*inputs)


def assemble_body(place, keep, received, own_field, other_field, full, field):
    first = place[0] == 0
    for xi in range(6):
        for yi in range(6):
            r = xi * 6 + yi
            for g in range(2):
                rows = pl.ds(g * 288 + r, 8, stride=36)
                a = keep[rows, :]
                b = received[rows, :]
                n = yi * 2 + g
                left = jnp.where(first, a, b)
                right = jnp.where(first, b, a)
                full[xi, n] = left
                full[6 + xi, n] = right
            a = jnp.broadcast_to(own_field[pl.ds(r, 1), :], (8, 128))
            b = jnp.broadcast_to(other_field[pl.ds(r, 1), :], (8, 128))
            field[xi, yi] = jnp.where(first, a, b)
            field[6 + xi, yi] = jnp.where(first, b, a)


def interior_body(alpha, shift, beta, full, field, *refs):
    acc = refs[-1]
    scaled = [-0.5 * alpha * w for w in weights]
    row = lax.broadcasted_iota(jnp.int32, (128, 128), 0)
    column = lax.broadcasted_iota(jnp.int32, (128, 128), 1)
    distance = jnp.abs(row - column)
    band = jnp.zeros((128, 128), F32)
    for k in range(1, 7):
        band = jnp.where(distance == k, F32(scaled[k]), band)
    band = jnp.where(distance == 0, F32(3.0 * scaled[0] - alpha * shift), band)
    for x in range(12):
        along = jnp.dot(
            full[x].reshape(96, 128), band, precision=lax.Precision.HIGHEST, preferred_element_type=F32
        ).reshape(12, 8, 128)
        for g in range(2):
            line = [full[x, yi * 2 + g] for yi in range(6)]
            for yi in range(6):
                n = yi * 2 + g
                total = along[n] + field[x, yi] * F32(alpha) * line[yi]
                for k in range(1, 7):
                    near = [line[yi + s] for s in (k, -k) if 0 <= yi + s < 6]
                    near += [full[x + s, n] for s in (k, -k) if 0 <= x + s < 12]
                    if near:
                        pair = near[0]
                        for v in near[1:]:
                            pair = pair + v
                        total = total + F32(scaled[k]) * pair
                if len(refs) == 2:
                    total = total - F32(beta) * refs[0][x, n]
                acc[x, n] = total


def edge_y_body(alpha, inside, acc, before, after, out):
    scaled = [-0.5 * alpha * w for w in weights]
    lower = [inside[2] * F32(s) for s in scaled]
    upper = [inside[3] * F32(s) for s in scaled]
    for x in range(12):
        for g in range(2):
            lows = [before[x, j * 2 + g] for j in range(6)]
            highs = [after[x, j * 2 + g] for j in range(6)]
            for yi in range(6):
                n = yi * 2 + g
                total = acc[x, n]
                for k in range(yi + 1, 7):
                    total = total + lower[k] * lows[6 + yi - k]
                for k in range(6 - yi, 7):
                    total = total + upper[k] * highs[yi + k - 6]
                out[x, n] = total


def edge_x_body(alpha, inside, acc, before, after, full, *halves):
    scaled = [-0.5 * alpha * w for w in weights]
    lower = [inside[0] * F32(s) for s in scaled]
    upper = [inside[1] * F32(s) for s in scaled]
    for n in range(12):
        lows = [before[j, n] for j in range(6)]
        highs = [after[j, n] for j in range(6)]
        for x in range(12):
            total = acc[x, n]
            if x < 6:
                for k in range(x + 1, 7):
                    total = total + lower[k] * lows[6 + x - k]
            else:
                for k in range(12 - x, 7):
                    total = total + upper[k] * highs[x + k - 12]
            full[x, n] = total
            if halves:
                halves[x // 6][x % 6, n] = total


def first_edge_body(alpha, inside, place, acc, keep_y, got_y, keep_x, got_x, full, low, high):
    scaled = [-0.5 * alpha * w for w in weights]
    from_x = [[inside[i] * F32(s) for s in scaled] for i in range(2)]
    from_y = [[inside[2 + i] * F32(s) for s in scaled] for i in range(2)]

    def with_order(first):
        before_x, after_x = (got_x, keep_x) if first else (keep_x, got_x)

        def rows(ref, xi, yi, g):
            return ref[pl.ds(g * 288 + xi * 6 + yi, 8, stride=36), :]

        for x in range(12):
            source = keep_y if (x < 6) == first else got_y
            for g in range(2):
                lows = [rows(source[0], x % 6, j, g) for j in range(6)]
                highs = [rows(source[1], x % 6, j, g) for j in range(6)]
                for yi in range(6):
                    n = yi * 2 + g
                    total = acc[x, n]
                    for k in range(yi + 1, 7):
                        total = total + from_y[0][k] * lows[6 + yi - k]
                    for k in range(6 - yi, 7):
                        total = total + from_y[1][k] * highs[yi + k - 6]
                    full[x, n] = total
        for g in range(2):
            for yi in range(6):
                n = yi * 2 + g
                lows = [rows(before_x, j, yi, g) for j in range(6)]
                highs = [rows(after_x, j, yi, g) for j in range(6)]
                for x in range(6):
                    total = full[x, n]
                    for k in range(x + 1, 7):
                        total = total + from_x[0][k] * lows[6 + x - k]
                    full[x, n] = total
                    low[x, n] = total
                    total = full[11 - x, n]
                    for k in range(x + 1, 7):
                        total = total + from_x[1][k] * highs[k - x - 1]
                    full[11 - x, n] = total
                    high[5 - x, n] = total

    pl.when(place[0] == 0)(lambda: with_order(True))
    pl.when(place[0] != 0)(lambda: with_order(False))


def bricks_body(place, low, high, following, preceding, out, rows, sem):
    first = place[0] == 0
    for xi in range(6):
        for yi in range(6):
            for g in range(2):
                n = yi * 2 + g
                start = g * 288 + xi * 6 + yi
                rows[pl.ds(start, 8, stride=36), :] = jnp.where(first, low[xi, n], preceding[6 + xi, n])
                rows[pl.ds(576 + start, 8, stride=36), :] = jnp.where(first, following[xi, n], high[xi, n])
    write = pltpu.make_async_copy(rows, out, sem)
    write.start()
    write.wait()


def stack(parts, half, xi, yi):
    left = [p[half][xi, yi * 2 + g] for p in parts for g in range(2)]
    right = [p[half][xi, yi * 2 + 2 + g] for p in parts for g in range(2)]
    return jnp.concatenate([jnp.concatenate(left, axis=0), jnp.concatenate(right, axis=0)], axis=1)


def products(left, right, halves=(0, 1)):
    total = None
    for half in halves:
        for xi in range(6):
            for yi in range(0, 6, 2):
                term = lax.dot_general(
                    stack(left, half, xi, yi),
                    stack(right, half, xi, yi),
                    (((1,), (1,)), ((), ())),
                    precision=lax.Precision.HIGHEST,
                    preferred_element_type=F32,
                )
                total = term if total is None else total + term
    return total


def halves_of(full):
    return full.at[pl.ds(0, 6)], full.at[pl.ds(6, 6)]


def near_gram_body(low, high, applied, following, preceding, out):
    mine = (low, high)
    total = products([mine, halves_of(applied)], [mine, halves_of(following), halves_of(preceding)])
    out[...] = jnp.concatenate([total, jnp.zeros((32, 80), F32)], axis=1)


def far_low_body(low, high, applied, far_low, out):
    far = products([(low, high), halves_of(applied)], [(far_low, None)], (0,))
    out[...] = jnp.concatenate([far, jnp.zeros((32, 112), F32)], axis=1)


def far_gram_body(place, low, high, applied, far_high, near, far_part, copies):
    far = far_part[:, 0:16] + products([(low, high), halves_of(applied)], [(None, far_high)], (1,))
    blocks = [near[:, 0:16], near[:, 16:32], far, near[:, 32:48]]
    total = None
    for p in range(4):
        turned = jnp.concatenate([blocks[(b - p) % 4] for b in range(4)], axis=1)
        total = turned if total is None else jnp.where(place[1] == p, turned, total)
    packed = jnp.concatenate([total[:16], total[16:]], axis=1)
    for n in range(16):
        copies[n] = packed


def sum_body(parts, copies):
    for half in range(2):
        total = parts[half * 8]
        for n in range(1, 8):
            total = total + parts[half * 8 + n]
        for n in range(8):
            copies[n, half * 16 : half * 16 + 16] = total


def finish_body(parts, energy, margin):
    total = parts[0]
    for n in range(1, 8):
        total = total + parts[n]
    total = total * F32(1.0 / CELLS)
    margin[...] = total[:, :64]
    energy[...] = total[:, 64:]


UP = [(i, (i + 1) % 8) for i in range(8)]
DOWN = [(i, (i + 7) % 8) for i in range(8)]
SWAP = [(0, 1), (1, 0)]
RING = ("xl", "xh")
SPOT = (0, 2, 1, 3)
NEXT = [(SPOT[i], SPOT[(i + 1) % 4]) for i in range(4)]
LAST = [(SPOT[i], SPOT[(i + 3) % 4]) for i in range(4)]
ROWS = ("y", "core")


def local(orbitals, potential):
    position_x = lax.axis_index("z")
    position_y = lax.axis_index(ROWS)
    side = lax.axis_index("xl")
    inside = jnp.stack([position_x > 0, position_x < 7, position_y > 0, position_y < 7]).astype(F32)
    place = jnp.stack([side, 2 * lax.axis_index("xh") + side]).astype(jnp.int32)

    half_width = (upper_edge - cut_edge) / 2.0
    centre = (upper_edge + cut_edge) / 2.0
    sigma_first = half_width / (lower_edge - centre)
    tau_value = 2.0 / sigma_first
    sigma_second = 1.0 / (tau_value - sigma_first)
    sigma_third = 1.0 / (tau_value - sigma_second)
    first = (sigma_first / half_width, centre, 0.0)
    second = (2.0 * sigma_second / half_width, centre, sigma_first * sigma_second)
    third = (2.0 * sigma_third / half_width, centre, sigma_second * sigma_third)
    plain = (1.0, 0.0, 0.0)

    mine = orbitals.reshape(1152, 128)
    own_field = potential.reshape(36, 128)
    keep = lax.dynamic_slice_in_dim(mine, side * 576, 576)
    received = lax.ppermute(lax.dynamic_slice_in_dim(mine, (1 - side) * 576, 576), "xl", SWAP)
    other_field = lax.ppermute(own_field, "xl", SWAP)

    def first_halos(values, way):
        along_x = [((z, s), ((z + (2 * s - 1) * way) % 8, s)) for z in range(8) for s in range(2)]
        along_x = [(2 * a + b, 2 * c + d) for (a, b), (c, d) in along_x]
        return (
            lax.ppermute(values, ("z", "xl"), along_x),
            lax.ppermute(values, ROWS, UP),
            lax.ppermute(values, ROWS, DOWN),
        )

    keep_x, *keep_y = first_halos(keep, 1)
    got_x, *got_y = first_halos(received, -1)
    full, field = call(
        assemble_body,
        [FULL, jax.ShapeDtypeStruct((12, 6, 8, 128), F32)],
        [place, keep, received, own_field, other_field],
        [SM] + [VM] * 4,
    )

    def first_interior(*refs):
        interior_body(*first, *refs)

    def first_edge(inside, place, acc, a, b, c, d, e, f, *outs):
        first_edge_body(first[0], inside, place, acc, (a, b), (c, d), e, f, *outs)

    acc = call(first_interior, FULL, [full, field], flops=400_000_000)
    y0 = (full,)
    y1 = call(
        first_edge,
        [FULL, HALF, HALF],
        [inside, place, acc, *keep_y, *got_y, keep_x, got_x],
        [SM, SM] + [VM] * 7,
    )

    def step(numbers, planes, previous, outs, last=False):
        full, low, high = planes
        before_x = lax.ppermute(high, "z", UP)
        after_x = lax.ppermute(low, "z", DOWN)
        later = full
        if last:
            later = lax.optimization_barrier((full, before_x))[0]
        halos = (lax.ppermute(full, ROWS, UP), lax.ppermute(later, ROWS, DOWN), before_x, after_x)

        def interior(*refs):
            interior_body(*numbers, *refs)

        acc = call(interior, FULL, [full, field, *previous], flops=400_000_000)

        def edge_y(*refs):
            edge_y_body(numbers[0], *refs)

        def edge_x(*refs):
            edge_x_body(numbers[0], *refs)

        acc = call(edge_y, FULL, [inside, acc, *halos[:2]], [SM] + [VM] * 3, flops=200_000_000)
        return call(edge_x, outs, [inside, acc, *halos[2:]], [SM] + [VM] * 3)

    y2 = step(second, y1, (y0[0],), [FULL, HALF, HALF])
    y3 = step(third, y2, (y1[0],), [FULL, HALF, HALF])
    full, low, high = y3
    following = lax.ppermute(full, RING, LAST)
    preceding = lax.ppermute(full, RING, NEXT)
    far_low = lax.ppermute(following[:6], RING, LAST)
    far_high = lax.ppermute(preceding[6:], RING, NEXT)
    applied = step(plain, y3, (), [FULL], True)[0]
    filtered = call(
        bricks_body,
        jax.ShapeDtypeStruct((1152, 128), F32),
        [place, low, high, following, preceding],
        [SM] + [VM] * 4,
        out_specs=pl.BlockSpec(memory_space=pl.ANY),
        scratch=[pltpu.VMEM((1152, 128), F32), pltpu.SemaphoreType.DMA],
        flops=400_000_000,
    )
    applied = lax.optimization_barrier((applied, filtered))[0]
    near = call(
        near_gram_body,
        jax.ShapeDtypeStruct((32, 128), F32),
        [low, high, applied, following, preceding],
        flops=400_000_000,
    )
    far_part = call(
        far_low_body,
        jax.ShapeDtypeStruct((32, 128), F32),
        [low, high, applied, far_low],
        flops=400_000_000,
    )
    copies = call(
        far_gram_body,
        jax.ShapeDtypeStruct((16, 16, 128), F32),
        [place, low, high, applied, far_high, near, far_part],
        [SM] + [VM] * 6,
    )
    parts = lax.all_to_all(copies, ("xl",) + ROWS, split_axis=0, concat_axis=0, tiled=True)
    copies = call(sum_body, jax.ShapeDtypeStruct((8, 32, 128), F32), [parts])
    parts = lax.all_to_all(copies, "z", split_axis=0, concat_axis=0, tiled=True)
    energy, margin = call(finish_body, [jax.ShapeDtypeStruct((32, 64), F32)] * 2, [parts])
    return filtered.reshape(32, 1, 6, 6, 128), energy, margin


def solution(mesh):
    fine = Mesh(mesh.devices.reshape(8, 2, 4, 2, 2), ("z", "xl", "y", "core", "xh"))
    brick = ("z", "xl", "y", "core")
    return jax.shard_map(
        local,
        mesh=fine,
        in_specs=(P("xh", brick, None, None, None), P(brick, None, None, None)),
        out_specs=(P("xh", brick, None, None, None), P("xh", None), P("xh", None)),
        check_vma=False,
    )
```

```python
import jax
import jax.numpy as jnp
from jax import lax
from jax.experimental import pallas as pl
from jax.experimental.pallas import tpu as pltpu
from jax.sharding import Mesh, PartitionSpec as P

weights = (
    -5369.0 / 1800.0,
    12.0 / 7.0,
    -15.0 / 56.0,
    10.0 / 189.0,
    -1.0 / 112.0,
    2.0 / 825.0,
    -1.0 / 4752.0,
)
lower_edge = 0.0
cut_edge = 3.0
upper_edge = 13.0
CELLS = 96 * 48 * 128

VM = pl.BlockSpec(memory_space=pltpu.VMEM)
SM = pl.BlockSpec(memory_space=pltpu.SMEM)
PARAMS = pltpu.CompilerParams(vmem_limit_bytes=8 * 1024 * 1024)
F32 = jnp.float32

HALF = jax.ShapeDtypeStruct((6, 12, 8, 128), F32)
FULL = jax.ShapeDtypeStruct((12, 12, 8, 128), F32)


def call(body, outs, inputs, specs=None, out_specs=None, scratch=(), flops=1_000_000):
    return pl.pallas_call(
        body,
        out_shape=outs,
        in_specs=specs or [VM] * len(inputs),
        out_specs=out_specs or jax.tree.map(lambda _: VM, outs),
        scratch_shapes=scratch,
        compiler_params=PARAMS,
        cost_estimate=pl.CostEstimate(flops=flops, bytes_accessed=2_000_000, transcendentals=0),
    )(*inputs)


def assemble_body(place, keep, received, own_field, other_field, full, field):
    first = place[0] == 0
    for xi in range(6):
        for yi in range(6):
            r = xi * 6 + yi
            for g in range(2):
                rows = pl.ds(g * 288 + r, 8, stride=36)
                a = keep[rows, :]
                b = received[rows, :]
                n = yi * 2 + g
                left = jnp.where(first, a, b)
                right = jnp.where(first, b, a)
                full[xi, n] = left
                full[6 + xi, n] = right
            a = jnp.broadcast_to(own_field[pl.ds(r, 1), :], (8, 128))
            b = jnp.broadcast_to(other_field[pl.ds(r, 1), :], (8, 128))
            field[xi, yi] = jnp.where(first, a, b)
            field[6 + xi, yi] = jnp.where(first, b, a)


def interior_body(alpha, shift, beta, full, field, *refs):
    acc = refs[-1]
    scaled = [-0.5 * alpha * w for w in weights]
    row = lax.broadcasted_iota(jnp.int32, (128, 128), 0)
    column = lax.broadcasted_iota(jnp.int32, (128, 128), 1)
    distance = jnp.abs(row - column)
    band = jnp.zeros((128, 128), F32)
    for k in range(1, 7):
        band = jnp.where(distance == k, F32(scaled[k]), band)
    band = jnp.where(distance == 0, F32(3.0 * scaled[0] - alpha * shift), band)
    for x in range(12):
        along = jnp.dot(
            full[x].reshape(96, 128), band, precision=lax.Precision.HIGHEST, preferred_element_type=F32
        ).reshape(12, 8, 128)
        for g in range(2):
            line = [full[x, yi * 2 + g] for yi in range(6)]
            for yi in range(6):
                n = yi * 2 + g
                total = along[n] + field[x, yi] * F32(alpha) * line[yi]
                for k in range(1, 7):
                    near = [line[yi + s] for s in (k, -k) if 0 <= yi + s < 6]
                    near += [full[x + s, n] for s in (k, -k) if 0 <= x + s < 12]
                    if near:
                        pair = near[0]
                        for v in near[1:]:
                            pair = pair + v
                        total = total + F32(scaled[k]) * pair
                if len(refs) == 2:
                    total = total - F32(beta) * refs[0][x, n]
                acc[x, n] = total


def edge_y_body(alpha, inside, acc, before, after, out):
    scaled = [-0.5 * alpha * w for w in weights]
    lower = [inside[2] * F32(s) for s in scaled]
    upper = [inside[3] * F32(s) for s in scaled]
    for x in range(12):
        for g in range(2):
            lows = [before[x, j * 2 + g] for j in range(6)]
            highs = [after[x, j * 2 + g] for j in range(6)]
            for yi in range(6):
                n = yi * 2 + g
                total = acc[x, n]
                for k in range(yi + 1, 7):
                    total = total + lower[k] * lows[6 + yi - k]
                for k in range(6 - yi, 7):
                    total = total + upper[k] * highs[yi + k - 6]
                out[x, n] = total


def edge_x_body(alpha, inside, acc, before, after, full, *halves):
    scaled = [-0.5 * alpha * w for w in weights]
    lower = [inside[0] * F32(s) for s in scaled]
    upper = [inside[1] * F32(s) for s in scaled]
    for n in range(12):
        lows = [before[j, n] for j in range(6)]
        highs = [after[j, n] for j in range(6)]
        for x in range(12):
            total = acc[x, n]
            if x < 6:
                for k in range(x + 1, 7):
                    total = total + lower[k] * lows[6 + x - k]
            else:
                for k in range(12 - x, 7):
                    total = total + upper[k] * highs[x + k - 12]
            full[x, n] = total
            if halves:
                halves[x // 6][x % 6, n] = total


def first_edge_body(alpha, inside, place, acc, keep_y, got_y, keep_x, got_x, full, low, high):
    scaled = [-0.5 * alpha * w for w in weights]
    from_x = [[inside[i] * F32(s) for s in scaled] for i in range(2)]
    from_y = [[inside[2 + i] * F32(s) for s in scaled] for i in range(2)]

    def with_order(first):
        before_x, after_x = (got_x, keep_x) if first else (keep_x, got_x)

        def rows(ref, xi, yi, g):
            return ref[pl.ds(g * 288 + xi * 6 + yi, 8, stride=36), :]

        for x in range(12):
            source = keep_y if (x < 6) == first else got_y
            for g in range(2):
                lows = [rows(source[0], x % 6, j, g) for j in range(6)]
                highs = [rows(source[1], x % 6, j, g) for j in range(6)]
                for yi in range(6):
                    n = yi * 2 + g
                    total = acc[x, n]
                    for k in range(yi + 1, 7):
                        total = total + from_y[0][k] * lows[6 + yi - k]
                    for k in range(6 - yi, 7):
                        total = total + from_y[1][k] * highs[yi + k - 6]
                    full[x, n] = total
        for g in range(2):
            for yi in range(6):
                n = yi * 2 + g
                lows = [rows(before_x, j, yi, g) for j in range(6)]
                highs = [rows(after_x, j, yi, g) for j in range(6)]
                for x in range(6):
                    total = full[x, n]
                    for k in range(x + 1, 7):
                        total = total + from_x[0][k] * lows[6 + x - k]
                    full[x, n] = total
                    low[x, n] = total
                    total = full[11 - x, n]
                    for k in range(x + 1, 7):
                        total = total + from_x[1][k] * highs[k - x - 1]
                    full[11 - x, n] = total
                    high[5 - x, n] = total

    pl.when(place[0] == 0)(lambda: with_order(True))
    pl.when(place[0] != 0)(lambda: with_order(False))


def bricks_body(place, low, high, following, preceding, out, rows, sem):
    first = place[0] == 0
    for xi in range(6):
        for yi in range(6):
            for g in range(2):
                n = yi * 2 + g
                start = g * 288 + xi * 6 + yi
                rows[pl.ds(start, 8, stride=36), :] = jnp.where(first, low[xi, n], preceding[6 + xi, n])
                rows[pl.ds(576 + start, 8, stride=36), :] = jnp.where(first, following[xi, n], high[xi, n])
    write = pltpu.make_async_copy(rows, out, sem)
    write.start()
    write.wait()


def stack(parts, half, xi, yi):
    left = [p[half][xi, yi * 2 + g] for p in parts for g in range(2)]
    right = [p[half][xi, yi * 2 + 2 + g] for p in parts for g in range(2)]
    return jnp.concatenate([jnp.concatenate(left, axis=0), jnp.concatenate(right, axis=0)], axis=1)


def products(left, right, halves=(0, 1)):
    total = None
    for half in halves:
        for xi in range(6):
            for yi in range(0, 6, 2):
                term = lax.dot_general(
                    stack(left, half, xi, yi),
                    stack(right, half, xi, yi),
                    (((1,), (1,)), ((), ())),
                    precision=lax.Precision.HIGHEST,
                    preferred_element_type=F32,
                )
                total = term if total is None else total + term
    return total


def halves_of(full):
    return full.at[pl.ds(0, 6)], full.at[pl.ds(6, 6)]


def near_gram_body(low, high, applied, following, preceding, out):
    mine = (low, high)
    total = products([mine, halves_of(applied)], [mine, halves_of(following), halves_of(preceding)])
    out[...] = jnp.concatenate([total, jnp.zeros((32, 80), F32)], axis=1)


def far_low_body(low, high, applied, far_low, out):
    far = products([(low, high), halves_of(applied)], [(far_low, None)], (0,))
    out[...] = jnp.concatenate([far, jnp.zeros((32, 112), F32)], axis=1)


def far_gram_body(place, low, high, applied, far_high, near, far_part, copies):
    far = far_part[:, 0:16] + products([(low, high), halves_of(applied)], [(None, far_high)], (1,))
    blocks = [near[:, 0:16], near[:, 16:32], far, near[:, 32:48]]
    total = None
    for p in range(4):
        turned = jnp.concatenate([blocks[(b - p) % 4] for b in range(4)], axis=1)
        total = turned if total is None else jnp.where(place[1] == p, turned, total)
    packed = jnp.concatenate([total[:16], total[16:]], axis=1)
    for n in range(16):
        copies[n] = packed


def sum_body(parts, copies):
    for half in range(2):
        total = parts[half * 8]
        for n in range(1, 8):
            total = total + parts[half * 8 + n]
        for n in range(8):
            copies[n, half * 16 : half * 16 + 16] = total


def finish_body(parts, energy, margin):
    total = parts[0]
    for n in range(1, 8):
        total = total + parts[n]
    total = total * F32(1.0 / CELLS)
    margin[...] = total[:, :64]
    energy[...] = total[:, 64:]


UP = [(i, (i + 1) % 8) for i in range(8)]
DOWN = [(i, (i + 7) % 8) for i in range(8)]
SWAP = [(0, 1), (1, 0)]
RING = ("xl", "xh")
SPOT = (0, 2, 1, 3)
NEXT = [(SPOT[i], SPOT[(i + 1) % 4]) for i in range(4)]
LAST = [(SPOT[i], SPOT[(i + 3) % 4]) for i in range(4)]
ROWS = ("y", "core")


def local(orbitals, potential):
    position_x = lax.axis_index("z")
    position_y = lax.axis_index(ROWS)
    side = lax.axis_index("xl")
    inside = jnp.stack([position_x > 0, position_x < 7, position_y > 0, position_y < 7]).astype(F32)
    place = jnp.stack([side, 2 * lax.axis_index("xh") + side]).astype(jnp.int32)

    half_width = (upper_edge - cut_edge) / 2.0
    centre = (upper_edge + cut_edge) / 2.0
    sigma_first = half_width / (lower_edge - centre)
    tau_value = 2.0 / sigma_first
    sigma_second = 1.0 / (tau_value - sigma_first)
    sigma_third = 1.0 / (tau_value - sigma_second)
    first = (sigma_first / half_width, centre, 0.0)
    second = (2.0 * sigma_second / half_width, centre, sigma_first * sigma_second)
    third = (2.0 * sigma_third / half_width, centre, sigma_second * sigma_third)
    plain = (1.0, 0.0, 0.0)

    mine = orbitals.reshape(1152, 128)
    own_field = potential.reshape(36, 128)
    keep = lax.dynamic_slice_in_dim(mine, side * 576, 576)
    received = lax.ppermute(lax.dynamic_slice_in_dim(mine, (1 - side) * 576, 576), "xl", SWAP)
    other_field = lax.ppermute(own_field, "xl", SWAP)

    def first_halos(values, way):
        along_x = [((z, s), ((z + (2 * s - 1) * way) % 8, s)) for z in range(8) for s in range(2)]
        along_x = [(2 * a + b, 2 * c + d) for (a, b), (c, d) in along_x]
        return (
            lax.ppermute(values, ("z", "xl"), along_x),
            lax.ppermute(values, ROWS, UP),
            lax.ppermute(values, ROWS, DOWN),
        )

    keep_x, *keep_y = first_halos(keep, 1)
    got_x, *got_y = first_halos(received, -1)
    full, field = call(
        assemble_body,
        [FULL, jax.ShapeDtypeStruct((12, 6, 8, 128), F32)],
        [place, keep, received, own_field, other_field],
        [SM] + [VM] * 4,
    )

    def first_interior(*refs):
        interior_body(*first, *refs)

    def first_edge(inside, place, acc, a, b, c, d, e, f, *outs):
        first_edge_body(first[0], inside, place, acc, (a, b), (c, d), e, f, *outs)

    acc = call(first_interior, FULL, [full, field], flops=400_000_000)
    y0 = (full,)
    y1 = call(
        first_edge,
        [FULL, HALF, HALF],
        [inside, place, acc, *keep_y, *got_y, keep_x, got_x],
        [SM, SM] + [VM] * 7,
    )

    def step(numbers, planes, previous, outs, last=False):
        full, low, high = planes
        def interior(*refs):
            interior_body(*numbers, *refs)

        before_x = lax.ppermute(high, "z", UP)
        after_x = lax.ppermute(low, "z", DOWN)
        acc = call(interior, FULL, [full, field, *previous], flops=400_000_000)
        later = full
        if last:
            later, acc, _ = lax.optimization_barrier((full, acc, before_x))
        halos = (lax.ppermute(full, ROWS, UP), lax.ppermute(later, ROWS, DOWN), before_x, after_x)

        def edge_y(*refs):
            edge_y_body(numbers[0], *refs)

        def edge_x(*refs):
            edge_x_body(numbers[0], *refs)

        acc = call(edge_y, FULL, [inside, acc, *halos[:2]], [SM] + [VM] * 3, flops=200_000_000)
        return call(edge_x, outs, [inside, acc, *halos[2:]], [SM] + [VM] * 3)

    y2 = step(second, y1, (y0[0],), [FULL, HALF, HALF])
    y3 = step(third, y2, (y1[0],), [FULL, HALF, HALF])
    full, low, high = y3
    following = lax.ppermute(full, RING, LAST)
    preceding = lax.ppermute(full, RING, NEXT)
    far_low = lax.ppermute(following[:6], RING, LAST)
    far_high = lax.ppermute(preceding[6:], RING, NEXT)
    applied = step(plain, y3, (), [FULL], True)[0]
    filtered = call(
        bricks_body,
        jax.ShapeDtypeStruct((1152, 128), F32),
        [place, low, high, following, preceding],
        [SM] + [VM] * 4,
        out_specs=pl.BlockSpec(memory_space=pl.ANY),
        scratch=[pltpu.VMEM((1152, 128), F32), pltpu.SemaphoreType.DMA],
        flops=400_000_000,
    )
    applied = lax.optimization_barrier((applied, filtered))[0]
    near = call(
        near_gram_body,
        jax.ShapeDtypeStruct((32, 128), F32),
        [low, high, applied, following, preceding],
        flops=400_000_000,
    )
    far_part = call(
        far_low_body,
        jax.ShapeDtypeStruct((32, 128), F32),
        [low, high, applied, far_low],
        flops=400_000_000,
    )
    copies = call(
        far_gram_body,
        jax.ShapeDtypeStruct((16, 16, 128), F32),
        [place, low, high, applied, far_high, near, far_part],
        [SM] + [VM] * 6,
    )
    parts = lax.all_to_all(copies, ("xl",) + ROWS, split_axis=0, concat_axis=0, tiled=True)
    copies = call(sum_body, jax.ShapeDtypeStruct((8, 32, 128), F32), [parts])
    parts = lax.all_to_all(copies, "z", split_axis=0, concat_axis=0, tiled=True)
    energy, margin = call(finish_body, [jax.ShapeDtypeStruct((32, 64), F32)] * 2, [parts])
    return filtered.reshape(32, 1, 6, 6, 128), energy, margin


def solution(mesh):
    fine = Mesh(mesh.devices.reshape(8, 2, 4, 2, 2), ("z", "xl", "y", "core", "xh"))
    brick = ("z", "xl", "y", "core")
    return jax.shard_map(
        local,
        mesh=fine,
        in_specs=(P("xh", brick, None, None, None), P(brick, None, None, None)),
        out_specs=(P("xh", brick, None, None, None), P("xh", None), P("xh", None)),
        check_vma=False,
    )
```
